32 devices in a mesh: row: 8 (over y, x, core), col: 4 (over z).
Axes of the slice: x: 2, y: 2, z: 4, core: 2. Of those that a mesh axis runs over, the one named last changes fastest.
Arguments:
- tiles: bfloat16 [8, 4, 80, 256, 256], P('row', 'col'), may hold values from -0.125 to 0.125
- tile_coords: int32 [2, 8, 4, 80], P(None, 'row', 'col'), may hold values from 0 to 1023, as said below
- tile_counts: int32 [8, 4], P('row', 'col'), may hold values from 40 to 80, as said below
- vectors: bfloat16 [262144, 16], P(('row', 'col')), may hold values from -6 to 6
Outputs:
- product: float32 [262144, 16], P(('row', 'col'))
The draws below stay inside these ranges and needn't reach their ends.
Inputs may be any that keep to these rules, and one draw needn't show every extreme that they name: `tile_coords`: for slot s below tile_counts[r, c]: the tile row I lies in r * 128 to (r + 1) * 128 - 1; the tile column J has (J // 32) % 4 equal to c; when I != J, I < J exactly when I + J is even; no (row, column) pair appears in two live slots anywhere. Among the live slots of one device at most 35 have tile rows in any one run of 32 tile rows, and at most 28 have tile columns in any one run of 32 tile columns; a device with all slots live reaches both. Slots at or above the count hold 0. `tile_counts`: some device holds exactly 80 live slots.
All inputs are finite; a program needn't handle non-finite values.
Results may differ from the reference program's by a relative error of at most 0.0075.
Values may be sent and summed in bfloat16 or wider, within the bound.
A program may use at most 320 MiB of HBM per device.

```python
import jax
import jax.numpy as jnp
from jax import lax

TILE = 256
VECS = 16
TPS = 32
TILES_DEV = 80
ORDER = 262144
N_ROW = 8
N_COL = 4


def owner_draw(sub_key, owners, dev_total):
    hot_slots = TILES_DEV // 4
    rounds = (TILES_DEV - hot_slots + owners - 1) // owners
    slot_ids = jnp.arange(TILES_DEV, dtype=jnp.int32)
    busiest = jax.random.randint(jax.random.fold_in(sub_key, 1), (dev_total,), 0, owners).astype(jnp.int32)
    scores = jax.random.randint(jax.random.fold_in(sub_key, 2), (dev_total, rounds, owners - 1), 0, 2 ** 20) * owners
    scores = scores + jnp.arange(owners - 1, dtype=jnp.int32)[None, None, :]
    orders = jnp.argsort(scores, axis=-1).astype(jnp.int32)
    others = orders + (orders >= busiest[:, None, None]).astype(jnp.int32)
    offset = jnp.maximum(slot_ids - hot_slots, 0)
    round_ids = offset // owners
    position = offset % owners
    picked = others[:, round_ids, jnp.maximum(position - 1, 0)]
    return jnp.where((position == 0)[None, :], busiest[:, None], picked).astype(jnp.int32)


def pattern_draw(key):
    key = jax.random.fold_in(key, 7)
    dev_total = N_ROW * N_COL
    row_span = TPS * N_COL
    half_cells = TPS * TPS // 2
    half_side = TPS // 2
    device_ids = jnp.arange(dev_total, dtype=jnp.int32)
    row_here = device_ids // N_COL
    col_here = device_ids % N_COL
    slot_ids = jnp.arange(TILES_DEV, dtype=jnp.int32)
    row_owner = owner_draw(jax.random.fold_in(key, 10), N_COL, dev_total)
    col_owner = owner_draw(jax.random.fold_in(key, 20), N_ROW, dev_total)
    earlier = (slot_ids[None, :] < slot_ids[:, None])[None]
    same_block = (row_owner[:, :, None] == row_owner[:, None, :]) & (col_owner[:, :, None] == col_owner[:, None, :]) & earlier
    rank = jnp.sum(same_block.astype(jnp.int32), axis=2)
    offsets = jax.random.randint(jax.random.fold_in(key, 3), (dev_total, N_COL, N_ROW), 0, half_cells).astype(jnp.int32)
    block_off = offsets[device_ids[:, None], row_owner, col_owner]
    cell_scores = jax.random.randint(jax.random.fold_in(key, 4), (dev_total, half_cells), 0, 2 ** 20) * half_cells
    cell_scores = cell_scores + jnp.arange(half_cells, dtype=jnp.int32)[None, :]
    cell_perm = jnp.argsort(cell_scores, axis=1).astype(jnp.int32)
    cells = jnp.take_along_axis(cell_perm, (rank + block_off) % half_cells, axis=1)
    inner_row = cells // half_side
    inner_pair = cells % half_side
    pick_rows = row_here[:, None] * row_span + row_owner * TPS + inner_row
    col_first = (col_owner * N_COL + col_here[:, None]) * TPS + 2 * inner_pair
    kept = (pick_rows == col_first) | ((pick_rows < col_first) == ((pick_rows + col_first) % 2 == 0))
    pick_cols = jnp.where(kept, col_first, col_first + 1)
    drawn = jax.random.randint(jax.random.fold_in(key, 5), (dev_total,), TILES_DEV // 2, TILES_DEV + 1)
    full_dev = jax.random.randint(jax.random.fold_in(key, 6), (), 0, dev_total)
    counts = jnp.where(device_ids == full_dev, TILES_DEV, drawn).astype(jnp.int32)
    live_slots = slot_ids[None, :] < counts[:, None]
    pick_rows = jnp.where(live_slots, pick_rows, 0).astype(jnp.int32)
    pick_cols = jnp.where(live_slots, pick_cols, 0).astype(jnp.int32)
    return (pick_rows, pick_cols, counts)


def draw_tile_coords(key, part):
    pick_rows, pick_cols, _ = pattern_draw(key)
    return jnp.stack([pick_rows, pick_cols]).reshape(2, N_ROW, N_COL, TILES_DEV)


def draw_tile_counts(key, part):
    _, _, counts = pattern_draw(key)
    return counts.reshape(N_ROW, N_COL)


def levels(rng, extent, pieces, low, largest):
    loudness, own = 1.0, jax.random.fold_in(rng, 6)
    for dim, blocks in pieces:
        steps = jnp.exp(jax.random.uniform(jax.random.fold_in(own, dim), (blocks,), jnp.float32, low / len(pieces), largest / len(pieces)))
        loudness = loudness * jnp.repeat(steps, extent[dim] // blocks).reshape([-1 if axis == dim else 1 for axis in range(len(extent))])
    return loudness


def gaussian(rng, extent, deviation, reach, cuts=(), kind=jnp.bfloat16):
    result = jax.random.normal(rng, extent, jnp.float32) * deviation
    if len(cuts) > 0:
        result = levels(rng, extent, cuts, -0.22, 0.18) * result
    return jnp.clip(result, min=-reach, max=reach).astype(kind)


def setup_inputs(seed: int = 0) -> dict:
    keys = jax.random.split(jax.random.key(seed), 5)
    return {
        "tiles": gaussian(keys[0], (N_ROW, N_COL, TILES_DEV, TILE, TILE), (8 * TILE) ** -0.5, 0.125, ((0, 8), (1, 4))),
        "tile_coords": draw_tile_coords(jax.random.fold_in(keys[4], 71), 0),
        "tile_counts": draw_tile_counts(jax.random.fold_in(keys[4], 71), 0),
        "vectors": gaussian(keys[3], (ORDER, VECS), 1.0, 6.0, ((0, 32),)),
    }


def split_tile(stored, tile_rows, tile_cols):
    size_tile = stored.shape[-1]
    down_idx = jnp.arange(size_tile, dtype=jnp.int32)[:, None]
    across_idx = jnp.arange(size_tile, dtype=jnp.int32)[None, :]
    off_diag = (tile_rows != tile_cols)[:, None, None]
    zero_val = jnp.zeros((), stored.dtype)
    upper_part = jnp.where(off_diag | (down_idx <= across_idx)[None], stored, zero_val)
    lower_part = jnp.where(off_diag | (down_idx < across_idx)[None], stored, zero_val)
    return upper_part, lower_part


def reference(tiles, tile_coords, tile_counts, vectors):
    dev_total = N_ROW * N_COL
    slot_count = tiles.shape[2]
    size_tile = tiles.shape[-1]
    vector_width = vectors.shape[1]
    vec_tiles = vectors.reshape(-1, size_tile, vector_width)
    flat_tiles = tiles.reshape(dev_total, slot_count, size_tile, size_tile)
    flat_rows = tile_coords[0].reshape(dev_total, slot_count).astype(jnp.int32)
    flat_cols = tile_coords[1].reshape(dev_total, slot_count).astype(jnp.int32)
    flat_counts = tile_counts.reshape(dev_total).astype(jnp.int32)

    def one_device(running, device_item):
        stored, tile_rows, tile_cols, live_count = device_item
        live_slots = jnp.arange(slot_count, dtype=jnp.int32) < live_count
        upper_part, lower_part = split_tile(stored, tile_rows, tile_cols)
        col_vecs = vec_tiles[tile_cols].astype(jnp.float32)
        row_vecs = vec_tiles[tile_rows].astype(jnp.float32)
        apply_operator = jnp.einsum("tab,tbv->tav", upper_part.astype(jnp.float32), col_vecs).astype(jnp.bfloat16)
        mirror = jnp.einsum("tba,tbv->tav", lower_part.astype(jnp.float32), row_vecs).astype(jnp.bfloat16)
        apply_operator = jnp.where(live_slots[:, None, None], apply_operator.astype(jnp.float32), jnp.float32(0.0))
        mirror = jnp.where(live_slots[:, None, None], mirror.astype(jnp.float32), jnp.float32(0.0))
        running = running.at[tile_rows].add(apply_operator)
        running = running.at[tile_cols].add(mirror)
        return running, None

    start_sum = jnp.zeros(vec_tiles.shape, jnp.float32)
    running, _ = lax.scan(one_device, start_sum, (flat_tiles, flat_rows, flat_cols, flat_counts))
    return running.reshape(-1, vector_width)
```

```python
import functools

import jax
import jax.numpy as jnp
from jax import lax
from jax.experimental import pallas as pl
from jax.experimental.pallas import tpu as pltpu
from jax.sharding import PartitionSpec as P

MESH = pl.DeviceIdType.MESH
VMEM_LIMIT = 48 * 1024 * 1024
GROUP = 8


def fused_kernel(
    coords_hbm, count_hbm, x_hbm, t_ref, o_ref,
    xv, xr, xc, upper, lower, tri, made, cum_f, cum_m, table_v,
    z_out, z_in, sib_out, sib_in, diag_out, diag_in, near_out, near_in,
    coords, coords_v, count_v, table,
    in_sem, tile_sem, zs, zr, ys, yr, ss, sr, ps, pr, bs, br, ds, dr, ns, nr,
):
    r, c = lax.axis_index("row"), lax.axis_index("col")
    chip, core = r // 2, r % 2
    cx, cy = chip % 2, chip // 2
    beside, across, opposite = 2 * cy + 1 - cx, 2 * (1 - cy) + cx, 3 - chip
    sib = 2 * chip + 1 - core
    xn, yn, dn = 2 * beside + core, 2 * across + core, 2 * opposite + core
    mid = (c == 1) | (c == 2)
    end = (c == 0) | (c == 3)
    next_mid = 1 + c // 3
    near_end, far_mid = 3 * (c - 1), 3 - c
    far_end = 3 - near_end
    slots, tile = upper.shape[0], upper.shape[1]
    vecs = x_hbm.shape[0]
    per_slab = x_hbm.shape[1] // tile
    half = per_slab // 2
    groups = slots // GROUP
    span = 4 * per_slab
    f32, bf16, i32 = jnp.float32, jnp.bfloat16, jnp.int32

    def part(k):
        return pl.ds(k * half, half)

    x_copy = pltpu.make_async_copy(x_hbm, xv, in_sem.at[0])
    coords_copy = pltpu.make_async_copy(coords_hbm, coords, in_sem.at[1])
    coords_v_copy = pltpu.make_async_copy(coords_hbm, coords_v, in_sem.at[2])
    count_copy = pltpu.make_async_copy(count_hbm, count_v, in_sem.at[3])
    table_copy = pltpu.make_async_copy(table_v, table, in_sem.at[4])
    for copy in (x_copy, coords_v_copy, count_copy, coords_copy):
        copy.start()

    def tile_copy(g):
        at = pl.ds(g * GROUP, GROUP)
        return pltpu.make_async_copy(t_ref.at[0, 0, at], lower.at[at], tile_sem.at[g])

    barrier = pltpu.get_barrier_semaphore()
    for row in (xn, yn, sib):
        pl.semaphore_signal(barrier, inc=1, device_id=(row, c), device_id_type=MESH)

    @pl.when(c > 0)
    def _():
        pl.semaphore_signal(barrier, inc=1, device_id=(r, c - 1), device_id_type=MESH)

    @pl.when(c < 3)
    def _():
        pl.semaphore_signal(barrier, inc=1, device_id=(r, c + 1), device_id_type=MESH)

    def start_tiles(g, _):
        tile_copy(g).start()
        return 0

    x_copy.wait()
    lax.fori_loop(0, groups, start_tiles, 0)
    for p in range(per_slab):
        xr[c, p] = xv[:, p * tile : (p + 1) * tile]

    @pl.when(mid)
    def _():
        pl.semaphore_wait(barrier, 5)

    @pl.when(end)
    def _():
        pl.semaphore_wait(barrier, 4)

    def remote(src, dst, send, recv, row, col):
        return pltpu.make_async_remote_copy(
            src, dst, send, recv, device_id=(row, col), device_id_type=MESH
        )

    def z_copy(j, owner, k, to):
        block = xr.at[owner, part(k)]
        return remote(block, block, zs.at[j, k], zr.at[owner, k], r, to)

    def link_half(link, first):
        return (0 if first else 1) if link == 0 else (1 if first else 0)

    links = (xn, yn)

    def own_copy(link, owner, i):
        k = link_half(link, i == 0)
        return remote(
            xr.at[c, part(k)], xc.at[owner, part(k)], ys.at[link, i], yr.at[link, i],
            links[link], c,
        )

    def pass_copy(link, owner):
        k = link_half(link, False)
        block = xc.at[owner, part(k)]
        return remote(block, block, ys.at[link, 2], yr.at[link, 2], links[link], c)

    def sib_copy(i, src, owner, k):
        return remote(src, xc.at[owner, part(k)], ss.at[i, k], sr.at[i, k], sib, c)

    def start_own(k):
        @pl.when(c < 3)
        def _():
            z_copy(0, c, k, c + 1).start()

        @pl.when(c > 0)
        def _():
            z_copy(1, c, k, c - 1).start()

        for link in range(2):
            own_copy(link, r, k).start()

    start_own(0)
    start_own(1)
    for k in range(2):
        sib_copy(0, xr.at[c, part(k)], r, k).start()
    for p in range(per_slab):
        xc[r, p] = xv[:, p * tile : (p + 1) * tile]

    coords_v_copy.wait()
    count_copy.wait()
    rows_v, cols_v = coords_v[0, 0], coords_v[1, 0]
    lane = lax.broadcasted_iota(i32, (slots, slots), 1)
    down = lax.broadcasted_iota(i32, (slots, slots), 0)
    live = lax.broadcasted_iota(i32, (1, slots), 1) < count_v[0:1, 0:1]
    places = (rows_v % span, cols_v // span * per_slab + cols_v % per_slab)
    width = table_v.shape[1]
    order = lax.broadcasted_iota(i32, (slots, width), 0) + 1
    target = lax.broadcasted_iota(i32, (slots, width), 1)
    for k in range(2):
        place = jnp.where(live, places[k], -1)
        tall = jnp.where(down == lane, jnp.broadcast_to(place, (slots, slots)), 0)
        tall = jnp.sum(tall.astype(f32), axis=1, keepdims=True).astype(i32)
        before = jnp.where((tall == place) & (down < lane), down + 1, 0)
        table_v[2 * k : 2 * k + 1, 0:slots] = jnp.max(before, axis=0, keepdims=True)
        found = jnp.where(tall == target, order, 0)
        table_v[2 * k + 1 : 2 * k + 2, :] = jnp.max(found, axis=0, keepdims=True)
    table_copy.start()
    cum_f[0] = jnp.zeros(cum_f.shape[1:], f32)
    cum_m[0] = jnp.zeros(cum_m.shape[1:], f32)

    down = lax.broadcasted_iota(i32, (tile, tile), 0)
    over = lax.broadcasted_iota(i32, (tile, tile), 1)
    tri[0] = (down <= over).astype(f32).astype(bf16)
    tri[1] = (down < over).astype(f32).astype(bf16)
    coords_copy.wait()

    def split_group(g, _):
        tile_copy(g).wait()
        for i in range(GROUP):
            s = g * GROUP + i
            gap = jnp.full((1, tile), coords[0, 0, 0, s] - coords[1, 0, 0, s], i32)
            off = jnp.minimum(gap * gap, 1).astype(f32).astype(bf16)
            stored = lower[s]
            upper[s] = stored * jnp.maximum(tri[0], off)
            lower[s] = stored * jnp.maximum(tri[1], off)
        return 0

    def split(a, b):
        lax.fori_loop(a * groups // 10, b * groups // 10, split_group, 0)

    def z_pass_one(k):
        @pl.when(mid)
        def _():
            z_copy(2, c - 1, k, c + 1).wait_recv()
            z_copy(2, c - 1, k, c + 1).start()
            z_copy(3, c + 1, k, c - 1).wait_recv()
            z_copy(3, c + 1, k, c - 1).start()

    def z_pass_two(k):
        @pl.when(mid)
        def _():
            z_copy(4, far_end, k, near_end).wait_recv()
            z_copy(4, far_end, k, near_end).start()

    split(0, 2)
    for link in range(2):
        own_copy(link, links[link], 0).wait_recv()
        pass_copy(1 - link, links[link]).start()
        k = link_half(link, True)
        sib_copy(1 + link, xc.at[links[link], part(k)], links[link], k).start()
    z_pass_one(0)
    split(2, 5)
    for link in range(2):
        own_copy(link, links[link], 1).wait_recv()
        k = link_half(link, False)
        sib_copy(1 + link, xc.at[links[link], part(k)], links[link], k).start()
    z_pass_one(1)
    split(5, 8)
    z_pass_two(0)
    split(8, 10)
    for link in range(2):
        pass_copy(link, dn).wait_recv()
        k = link_half(link, False)
        sib_copy(3, xc.at[dn, part(k)], dn, k).start()
    z_pass_two(1)
    table_copy.wait()
    for i, owner in enumerate((sib, 2 * beside + 1 - core, 2 * across + 1 - core,
                               2 * opposite + 1 - core)):
        for k in range(2):
            sib_copy(i, xc.at[owner, part(k)], owner, k).wait_recv()

    def running_sums(make, cum, at):
        def link(g):
            for i in range(GROUP):
                s = g * GROUP + i
                cum[s + 1] = made[s] + cum[table[at, s]]

        def group(g, _):
            for i in range(GROUP):
                make(g * GROUP + i)
            link(g - 1)
            return 0

        for i in range(GROUP):
            make(i)
        lax.fori_loop(1, groups, group, 0)
        link(groups - 1)

    def forward(s):
        col = coords[1, 0, 0, s]
        at = lax.div(col, span) * per_slab + lax.rem(col, per_slab)
        made[s] = lax.dot_general(
            xc[lax.div(at, per_slab), lax.rem(at, per_slab)], upper[s],
            (((1,), (1,)), ((), ())), preferred_element_type=f32,
        )

    def mirror(s):
        row = lax.rem(coords[0, 0, 0, s], span)
        made[s] = jnp.dot(
            xr[lax.div(row, per_slab), lax.rem(row, per_slab)], lower[s],
            preferred_element_type=f32,
        )

    def fill(dst, cum, at, owner, k, *more, to=None):
        base = k * half

        def body(i, _):
            out = cum[table[at, owner * per_slab + base + i]]
            for source, offset in more:
                out = out + source[offset + i].astype(f32)
            dst[(base if to is None else to) + i] = out.astype(dst.dtype)
            return 0

        lax.fori_loop(0, half, body, 0, unroll=8)

    def near(i, k):
        return remote(
            z_out.at[i, part(k)], z_in.at[i, part(k)], ps.at[i, k], pr.at[i, k], r, next_mid
        )

    def far(i, k):
        return remote(
            z_out.at[i, part(k)], z_in.at[3 + i, part(k)], ps.at[i, k], pr.at[3 + i, k],
            r, far_mid,
        )

    def to_end(k):
        return remote(
            z_out.at[2, part(k)], z_in.at[0, part(k)], ps.at[2, k], pr.at[0, k], r, near_end
        )

    def chain_far(i, k):
        @pl.when(mid)
        def _():
            near(i, k).wait_recv()
            owner = far_end if i == 0 else far_mid
            fill(z_out.at[i], cum_f, 1, owner, k, (z_in.at[i], k * half))
            far(i, k).start()

    def chain_end(k):
        @pl.when(mid)
        def _():
            far(0, k).wait_recv()
            fill(z_out.at[2], cum_f, 1, near_end, k, (z_in.at[3], k * half))
            to_end(k).start()

    def to_sib(j):
        return remote(sib_out.at[j], sib_in.at[j], bs.at[j], br.at[j], sib, c)

    def diag(link):
        return remote(
            diag_out.at[link], diag_in.at[link], ds.at[link], dr.at[link], links[link], c
        )

    def beside_copy(link, i):
        k = link_half(link, i == 0)
        return remote(
            near_out.at[link, part(k)], near_in.at[link, part(k)],
            ns.at[link, i], nr.at[link, i], links[link], c,
        )

    running_sums(forward, cum_f, 0)

    @pl.when(end)
    def _():
        for i, owner in enumerate((3 - c, 3 - next_mid, next_mid)):
            for k in range(2):
                fill(z_out.at[i], cum_f, 1, owner, k)
                near(i, k).start()

        def last_blocks(d, _):
            owner = jnp.where(c == 0, d, 3 - d)
            for k in range(2):
                z_copy(0, owner, k, next_mid).wait_recv()
            return 0

        lax.fori_loop(1, 4, last_blocks, 0)

    running_sums(mirror, cum_m, 2)
    for j, to in enumerate((opposite, beside, across, chip)):
        for k in range(2):
            fill(sib_out.at[j], cum_m, 3, 2 * to + 1 - core, k)
        to_sib(j).start()
    chain_far(0, 0)
    to_sib(0).wait_recv()
    for link in range(2):
        fill(diag_out.at[link], cum_m, 3, dn, link, (sib_in.at[0], link * half), to=0)
        diag(link).start()
    for link in range(2):
        to_sib(1 + link).wait_recv()
        k = link_half(link, True)
        fill(near_out.at[link], cum_m, 3, links[link], k, (sib_in.at[1 + link], k * half))
        beside_copy(link, 0).start()
    chain_far(0, 1)
    for link in range(2):
        diag(1 - link).wait_recv()
        k = link_half(link, False)
        fill(
            near_out.at[link], cum_m, 3, links[link], k,
            (sib_in.at[1 + link], k * half), (diag_in.at[1 - link], 0),
        )
        beside_copy(link, 1).start()
    chain_end(0)
    chain_far(1, 0)
    chain_end(1)
    to_sib(3).wait_recv()

    def blocks(body, a, b):
        def step(p, _):
            body(p, pl.ds(pl.multiple_of(p * tile, tile), tile))
            return 0

        lax.fori_loop(a, b, step, 0, unroll=8)

    def base(p, at):
        o_ref[:, at] = (
            cum_f[table[1, c * per_slab + p]] + cum_m[table[3, r * per_slab + p]]
            + sib_in[3, p].astype(f32)
        )

    def add(k, *sources):
        def body(p, at):
            out = o_ref[:, at]
            for source in sources:
                out = out + source[p].astype(f32)
            o_ref[:, at] = out

        blocks(body, k * half, (k + 1) * half)

    blocks(base, 0, per_slab)

    @pl.when(end)
    def _():
        for k in range(2):
            to_end(k).wait_recv()
            add(k, z_in.at[0])

    chain_far(1, 1)
    for link in range(2):
        beside_copy(link, 0).wait_recv()
        add(link_half(link, True), near_in.at[link])
    for link in range(2):
        beside_copy(link, 1).wait_recv()
        add(link_half(link, False), near_in.at[link])

    @pl.when(mid)
    def _():
        for k in range(2):
            far(1, k).wait_recv()
            near(2, k).wait_recv()
            add(k, z_in.at[4], z_in.at[2])

    for k in range(2):

        @pl.when(c < 3)
        def _():
            z_copy(0, c, k, c + 1).wait_send()

        @pl.when(c > 0)
        def _():
            z_copy(1, c, k, c - 1).wait_send()

        @pl.when(mid)
        def _():
            z_copy(2, c - 1, k, c + 1).wait_send()
            z_copy(3, c + 1, k, c - 1).wait_send()
            z_copy(4, far_end, k, near_end).wait_send()

        for i in range(3):
            near(i, k).wait_send()
        for link in range(2):
            own_copy(link, r, k).wait_send()
            beside_copy(link, k).wait_send()
        for i, owner in enumerate((r, xn, yn, dn)):
            sib_copy(i, xc.at[owner, part(k)], owner, k).wait_send()
    for link in range(2):
        pass_copy(link, links[1 - link]).wait_send()
        diag(link).wait_send()
    for j in range(4):
        to_sib(j).wait_send()


def fused(tiles, tile_coords, tile_counts, x):
    slots, tile = tiles.shape[2], tiles.shape[-1]
    vecs, width = x.shape
    slab = width // tile
    half = slab // 2
    dma, bf16, f32, i32 = pltpu.SemaphoreType.DMA, jnp.bfloat16, jnp.float32, jnp.int32

    def blocks(*lead, dtype=bf16):
        return pltpu.VMEM((*lead, vecs, tile), dtype)

    return pl.pallas_call(
        fused_kernel,
        out_shape=jax.ShapeDtypeStruct(x.shape, f32),
        in_specs=[pl.BlockSpec(memory_space=pltpu.HBM)] * 4,
        out_specs=pl.BlockSpec(memory_space=pltpu.VMEM),
        scratch_shapes=[
            pltpu.VMEM(x.shape, bf16),
            blocks(4, slab),
            blocks(8, slab),
            pltpu.VMEM((slots, tile, tile), bf16),
            pltpu.VMEM((slots, tile, tile), bf16),
            pltpu.VMEM((2, tile, tile), bf16),
            blocks(slots, dtype=f32),
            blocks(slots + 1, dtype=f32),
            blocks(slots + 1, dtype=f32),
            pltpu.VMEM((8, 8 * slab), i32),
            blocks(3, slab),
            blocks(5, slab),
            blocks(4, slab),
            blocks(4, slab),
            blocks(2, half),
            blocks(2, half),
            blocks(2, slab),
            blocks(2, slab),
            pltpu.SMEM(tile_coords.shape, i32),
            pltpu.VMEM(tile_coords.shape, i32),
            pltpu.VMEM((1, 1), i32),
            pltpu.SMEM((8, 8 * slab), i32),
            dma((5,)),
            dma((slots // GROUP,)),
            dma((5, 2)), dma((4, 2)),
            dma((2, 3)), dma((2, 3)),
            dma((4, 2)), dma((4, 2)),
            dma((3, 2)), dma((5, 2)),
            dma((4,)), dma((4,)),
            dma((2,)), dma((2,)),
            dma((2, 2)), dma((2, 2)),
        ],
        compiler_params=pltpu.CompilerParams(
            collective_id=0, has_side_effects=True, vmem_limit_bytes=VMEM_LIMIT
        ),
        name="fused_product",
    )(tile_coords, tile_counts, x, tiles)


def apply_kernel(
    slots, tile, per_slab, n_cols, coords, count,
    t_ref, xr_ref, xc_ref, f_ref, m_ref, facc, macc,
):
    step = pl.program_id(0)
    group = t_ref.shape[2]

    @pl.when(step == 0)
    def _():
        facc[...] = jnp.zeros_like(facc)
        macc[...] = jnp.zeros_like(macc)

    def place(s):
        tile_row, tile_col = coords[s], coords[slots + s]
        local = tile_row % (per_slab * n_cols)
        row_at = (local // per_slab, pl.multiple_of(local % per_slab * tile, tile))
        col_at = (
            tile_col // (per_slab * n_cols), pl.multiple_of(tile_col % per_slab * tile, tile),
        )
        return row_at, col_at

    def run(masked):
        made = []
        for g in range(group):
            s = step * group + g
            (ro, rp), (co, cp) = place(s)
            x_row = xr_ref[ro, :, pl.ds(rp, tile)]
            x_col = xc_ref[co, :, pl.ds(cp, tile)]
            upper = lower = t_ref[0, 0, g]
            if masked:
                off = coords[s] != coords[slots + s]
                down = lax.broadcasted_iota(jnp.int32, (tile, tile), 0)
                down = jnp.where(off, -1, down)
                across = lax.broadcasted_iota(jnp.int32, (tile, tile), 1)
                stored = upper.astype(jnp.float32)
                upper = jnp.where(down <= across, stored, 0.0).astype(jnp.bfloat16)
                lower = jnp.where(down < across, stored, 0.0).astype(jnp.bfloat16)
            forward = lax.dot_general(
                x_col, upper, (((1,), (1,)), ((), ())), preferred_element_type=jnp.float32
            )
            mirror = lax.dot_general(
                x_row, lower, (((1,), (0,)), ((), ())), preferred_element_type=jnp.float32
            )
            if masked:
                live = s < count[0]
                forward = jnp.where(live, forward, 0.0)
                mirror = jnp.where(live, mirror, 0.0)
            made.append((forward, mirror))
        for g in range(group):
            (ro, rp), (co, cp) = place(step * group + g)
            forward, mirror = made[g]
            facc[ro, :, pl.ds(rp, tile)] += forward
            macc[co, :, pl.ds(cp, tile)] += mirror

    special = coords[step * group] == coords[slots + step * group]
    for g in range(1, group):
        s = step * group + g
        special = special | (coords[s] == coords[slots + s])
    special = special | (step * group + group > count[0])

    @pl.when(special)
    def _():
        run(True)

    @pl.when(jnp.logical_not(special))
    def _():
        run(False)

    @pl.when(step == pl.num_programs(0) - 1)
    def _():
        f_ref[...] = facc[...].astype(f_ref.dtype)
        m_ref[...] = macc[...].astype(m_ref.dtype)


def apply_tiles(tiles, coords, count, xr, xc, tile):
    slots = tiles.shape[2]
    group = GROUP if slots % GROUP == 0 else 1
    n_cols = xr.shape[0]
    per_slab = xr.shape[2] // tile
    whole = lambda a: pl.BlockSpec(a.shape, lambda i, *_: (0, 0, 0))
    return pl.pallas_call(
        functools.partial(apply_kernel, slots, tile, per_slab, n_cols),
        out_shape=(
            jax.ShapeDtypeStruct(xr.shape, jnp.bfloat16),
            jax.ShapeDtypeStruct(xc.shape, jnp.bfloat16),
        ),
        grid_spec=pltpu.PrefetchScalarGridSpec(
            num_scalar_prefetch=2,
            grid=(slots // group,),
            in_specs=[
                pl.BlockSpec((1, 1, group, tile, tile), lambda i, *_: (0, 0, i, 0, 0)),
                whole(xr),
                whole(xc),
            ],
            out_specs=(whole(xr), whole(xc)),
            scratch_shapes=[
                pltpu.VMEM(xr.shape, jnp.float32),
                pltpu.VMEM(xc.shape, jnp.float32),
            ],
        ),
        compiler_params=pltpu.CompilerParams(vmem_limit_bytes=VMEM_LIMIT),
        name="apply_tiles",
    )(coords, count, tiles, xr, xc)


def shards(n_rows, n_cols, tiles, tile_coords, tile_counts, vectors):
    tile = tiles.shape[-1]
    x = vectors.T
    if (n_rows, n_cols) == (8, 4):
        return fused(tiles, tile_coords, tile_counts, x).T
    coords, count = tile_coords.reshape(-1), tile_counts.reshape(-1)
    xr = lax.all_gather(x, "col", axis=0)
    xc = lax.all_gather(x, "row", axis=0)
    f, m = apply_tiles(tiles, coords, count, xr, xc, tile)
    f = lax.all_to_all(f, "col", 0, 0, tiled=True)
    m = lax.all_to_all(m, "row", 0, 0, tiled=True)
    return (jnp.sum(f.astype(jnp.float32), 0) + jnp.sum(m.astype(jnp.float32), 0)).T


def solution(mesh):
    in_specs = (
        P("row", "col", None, None, None),
        P(None, "row", "col", None),
        P("row", "col"),
        P(("row", "col"), None),
    )
    out_specs = P(("row", "col"), None)
    body = functools.partial(shards, mesh.shape["row"], mesh.shape["col"])
    return jax.shard_map(body, mesh=mesh, in_specs=in_specs, out_specs=out_specs, check_vma=False)
```

```python
import functools

import jax
import jax.numpy as jnp
from jax import lax
from jax.experimental import pallas as pl
from jax.experimental.pallas import tpu as pltpu
from jax.sharding import PartitionSpec as P

MESH = pl.DeviceIdType.MESH
VMEM_LIMIT = 48 * 1024 * 1024
GROUP = 8
STEP = 40


def fused_kernel(
    coords_hbm, count_hbm, x_hbm, t_ref, o_ref,
    xv, xr, xc, upper, lower, tri, made, cum_f, cum_m, table_v,
    z_out, z_in, sib_out, sib_in, diag_out, diag_in, near_out, near_in,
    coords, coords_v, count_v, table,
    in_sem, tile_sem, zs, zr, ys, yr, ss, sr, ps, pr, bs, br, ds, dr, ns, nr,
):
    r, c = lax.axis_index("row"), lax.axis_index("col")
    chip, core = r // 2, r % 2
    cx, cy = chip % 2, chip // 2
    beside, across, opposite = 2 * cy + 1 - cx, 2 * (1 - cy) + cx, 3 - chip
    sib = 2 * chip + 1 - core
    xn, yn, dn = 2 * beside + core, 2 * across + core, 2 * opposite + core
    mid = (c == 1) | (c == 2)
    end = (c == 0) | (c == 3)
    next_mid = 1 + c // 3
    near_end, far_mid = 3 * (c - 1), 3 - c
    far_end = 3 - near_end
    slots, tile = upper.shape[0], upper.shape[1]
    vecs = x_hbm.shape[0]
    per_slab = x_hbm.shape[1] // tile
    half = per_slab // 2
    groups = slots // GROUP
    span = 4 * per_slab
    f32, bf16, i32 = jnp.float32, jnp.bfloat16, jnp.int32

    def part(k):
        return pl.ds(k * half, half)

    x_copy = pltpu.make_async_copy(x_hbm, xv, in_sem.at[0])
    coords_copy = pltpu.make_async_copy(coords_hbm, coords, in_sem.at[1])
    coords_v_copy = pltpu.make_async_copy(coords_hbm, coords_v, in_sem.at[2])
    count_copy = pltpu.make_async_copy(count_hbm, count_v, in_sem.at[3])
    table_copy = pltpu.make_async_copy(table_v, table, in_sem.at[4])
    for copy in (x_copy, coords_v_copy, count_copy, coords_copy):
        copy.start()

    def tile_copy(g):
        at = pl.ds(g * GROUP, GROUP)
        return pltpu.make_async_copy(t_ref.at[0, 0, at], lower.at[at], tile_sem.at[g])

    barrier = pltpu.get_barrier_semaphore()
    for row in (xn, yn, sib):
        pl.semaphore_signal(barrier, inc=1, device_id=(row, c), device_id_type=MESH)

    @pl.when(c > 0)
    def _():
        pl.semaphore_signal(barrier, inc=1, device_id=(r, c - 1), device_id_type=MESH)

    @pl.when(c < 3)
    def _():
        pl.semaphore_signal(barrier, inc=1, device_id=(r, c + 1), device_id_type=MESH)

    def start_tiles(g, _):
        tile_copy(g).start()
        return 0

    x_copy.wait()
    lax.fori_loop(0, groups, start_tiles, 0)
    for p in range(per_slab):
        xr[c, p] = xv[:, p * tile : (p + 1) * tile]

    @pl.when(mid)
    def _():
        pl.semaphore_wait(barrier, 5)

    @pl.when(end)
    def _():
        pl.semaphore_wait(barrier, 4)

    def remote(src, dst, send, recv, row, col):
        return pltpu.make_async_remote_copy(
            src, dst, send, recv, device_id=(row, col), device_id_type=MESH
        )

    def z_copy(j, owner, k, to):
        block = xr.at[owner, part(k)]
        return remote(block, block, zs.at[j, k], zr.at[owner, k], r, to)

    def link_half(link, first):
        return (0 if first else 1) if link == 0 else (1 if first else 0)

    links = (xn, yn)

    def own_copy(link, owner, i):
        k = link_half(link, i == 0)
        return remote(
            xr.at[c, part(k)], xc.at[owner, part(k)], ys.at[link, i], yr.at[link, i],
            links[link], c,
        )

    def pass_copy(link, owner):
        k = link_half(link, False)
        block = xc.at[owner, part(k)]
        return remote(block, block, ys.at[link, 2], yr.at[link, 2], links[link], c)

    def sib_copy(i, src, owner, k):
        return remote(src, xc.at[owner, part(k)], ss.at[i, k], sr.at[i, k], sib, c)

    def start_own(k):
        @pl.when(c < 3)
        def _():
            z_copy(0, c, k, c + 1).start()

        @pl.when(c > 0)
        def _():
            z_copy(1, c, k, c - 1).start()

        for link in range(2):
            own_copy(link, r, k).start()

    start_own(0)
    start_own(1)
    for k in range(2):
        sib_copy(0, xr.at[c, part(k)], r, k).start()
    for p in range(per_slab):
        xc[r, p] = xv[:, p * tile : (p + 1) * tile]

    coords_v_copy.wait()
    count_copy.wait()
    rows_v, cols_v = coords_v[0, 0], coords_v[1, 0]
    lane = lax.broadcasted_iota(i32, (slots, slots), 1)
    down = lax.broadcasted_iota(i32, (slots, slots), 0)
    live = lax.broadcasted_iota(i32, (1, slots), 1) < count_v[0:1, 0:1]
    places = (rows_v % span, cols_v // span * per_slab + cols_v % per_slab)
    width = table_v.shape[1]
    order = lax.broadcasted_iota(i32, (slots, width), 0) + 1
    target = lax.broadcasted_iota(i32, (slots, width), 1)
    for k in range(2):
        place = jnp.where(live, places[k], -1)
        tall = jnp.where(down == lane, jnp.broadcast_to(place, (slots, slots)), 0)
        tall = jnp.sum(tall.astype(f32), axis=1, keepdims=True).astype(i32)
        before = jnp.where((tall == place) & (down < lane), down + 1, 0)
        table_v[2 * k : 2 * k + 1, 0:slots] = jnp.max(before, axis=0, keepdims=True)
        found = jnp.where(tall == target, order, 0)
        table_v[2 * k + 1 : 2 * k + 2, :] = jnp.max(found, axis=0, keepdims=True)
    table_copy.start()
    cum_f[0] = jnp.zeros(cum_f.shape[1:], f32)
    cum_m[0] = jnp.zeros(cum_m.shape[1:], f32)

    down = lax.broadcasted_iota(i32, (tile, tile), 0)
    over = lax.broadcasted_iota(i32, (tile, tile), 1)
    tri[0] = (down >= over).astype(f32).astype(bf16)
    tri[1] = (down < over).astype(f32).astype(bf16)
    coords_copy.wait()

    def split_group(g, _):
        tile_copy(g).wait()
        for i in range(GROUP):
            s = g * GROUP + i
            gap = jnp.full((1, tile), coords[0, 0, 0, s] - coords[1, 0, 0, s], i32)
            off = jnp.minimum(gap * gap, 1).astype(f32).astype(bf16)
            stored = lower[s]
            upper[s] = stored.T * jnp.maximum(tri[0], off)
            lower[s] = stored * jnp.maximum(tri[1], off)
        return 0

    def split(a, b):
        lax.fori_loop(a * groups // 10, b * groups // 10, split_group, 0)

    def z_pass_one(k):
        @pl.when(mid)
        def _():
            z_copy(2, c - 1, k, c + 1).wait_recv()
            z_copy(2, c - 1, k, c + 1).start()
            z_copy(3, c + 1, k, c - 1).wait_recv()
            z_copy(3, c + 1, k, c - 1).start()

    def z_pass_two(k):
        @pl.when(mid)
        def _():
            z_copy(4, far_end, k, near_end).wait_recv()
            z_copy(4, far_end, k, near_end).start()

    split(0, 2)
    for link in range(2):
        own_copy(link, links[link], 0).wait_recv()
        pass_copy(1 - link, links[link]).start()
        k = link_half(link, True)
        sib_copy(1 + link, xc.at[links[link], part(k)], links[link], k).start()
    z_pass_one(0)
    split(2, 5)
    for link in range(2):
        own_copy(link, links[link], 1).wait_recv()
        k = link_half(link, False)
        sib_copy(1 + link, xc.at[links[link], part(k)], links[link], k).start()
    z_pass_one(1)
    split(5, 8)
    z_pass_two(0)
    split(8, 10)
    for link in range(2):
        pass_copy(link, dn).wait_recv()
        k = link_half(link, False)
        sib_copy(3, xc.at[dn, part(k)], dn, k).start()
    z_pass_two(1)
    table_copy.wait()
    for i, owner in enumerate((sib, 2 * beside + 1 - core, 2 * across + 1 - core,
                               2 * opposite + 1 - core)):
        for k in range(2):
            sib_copy(i, xc.at[owner, part(k)], owner, k).wait_recv()

    def running_sums(make, cum, at):
        def link(g):
            for i in range(STEP):
                s = g * STEP + i
                cum[s + 1] = made[s] + cum[table[at, s]]

        def group(g, _):
            for i in range(STEP):
                make(g * STEP + i)
            link(g - 1)
            return 0

        for i in range(STEP):
            make(i)
        lax.fori_loop(1, slots // STEP, group, 0)
        link(slots // STEP - 1)

    def forward(s):
        col = coords[1, 0, 0, s]
        at = lax.div(col, span) * per_slab + lax.rem(col, per_slab)
        made[s] = jnp.dot(
            xc[lax.div(at, per_slab), lax.rem(at, per_slab)], upper[s],
            preferred_element_type=f32,
        )

    def mirror(s):
        row = lax.rem(coords[0, 0, 0, s], span)
        made[s] = jnp.dot(
            xr[lax.div(row, per_slab), lax.rem(row, per_slab)], lower[s],
            preferred_element_type=f32,
        )

    def fill(dst, cum, at, owner, k, *more, to=None):
        base = k * half

        def body(i, _):
            out = cum[table[at, owner * per_slab + base + i]]
            for source, offset in more:
                out = out + source[offset + i].astype(f32)
            dst[(base if to is None else to) + i] = out.astype(dst.dtype)
            return 0

        lax.fori_loop(0, half, body, 0, unroll=8)

    def near(i, k):
        return remote(
            z_out.at[i, part(k)], z_in.at[i, part(k)], ps.at[i, k], pr.at[i, k], r, next_mid
        )

    def far(i, k):
        return remote(
            z_out.at[i, part(k)], z_in.at[3 + i, part(k)], ps.at[i, k], pr.at[3 + i, k],
            r, far_mid,
        )

    def to_end(k):
        return remote(
            z_out.at[2, part(k)], z_in.at[0, part(k)], ps.at[2, k], pr.at[0, k], r, near_end
        )

    def chain_far(i, k):
        @pl.when(mid)
        def _():
            near(i, k).wait_recv()
            owner = far_end if i == 0 else far_mid
            fill(z_out.at[i], cum_f, 1, owner, k, (z_in.at[i], k * half))
            far(i, k).start()

    def chain_end(k):
        @pl.when(mid)
        def _():
            far(0, k).wait_recv()
            fill(z_out.at[2], cum_f, 1, near_end, k, (z_in.at[3], k * half))
            to_end(k).start()

    def to_sib(j):
        return remote(sib_out.at[j], sib_in.at[j], bs.at[j], br.at[j], sib, c)

    def diag(link):
        return remote(
            diag_out.at[link], diag_in.at[link], ds.at[link], dr.at[link], links[link], c
        )

    def beside_copy(link, i):
        k = link_half(link, i == 0)
        return remote(
            near_out.at[link, part(k)], near_in.at[link, part(k)],
            ns.at[link, i], nr.at[link, i], links[link], c,
        )

    running_sums(forward, cum_f, 0)

    @pl.when(end)
    def _():
        for i, owner in enumerate((3 - c, 3 - next_mid, next_mid)):
            for k in range(2):
                fill(z_out.at[i], cum_f, 1, owner, k)
                near(i, k).start()

        def last_blocks(d, _):
            owner = jnp.where(c == 0, d, 3 - d)
            for k in range(2):
                z_copy(0, owner, k, next_mid).wait_recv()
            return 0

        lax.fori_loop(1, 4, last_blocks, 0)

    running_sums(mirror, cum_m, 2)
    for j, to in enumerate((opposite, beside, across, chip)):
        for k in range(2):
            fill(sib_out.at[j], cum_m, 3, 2 * to + 1 - core, k)
        to_sib(j).start()
    chain_far(0, 0)
    to_sib(0).wait_recv()
    for link in range(2):
        fill(diag_out.at[link], cum_m, 3, dn, link, (sib_in.at[0], link * half), to=0)
        diag(link).start()
    for link in range(2):
        to_sib(1 + link).wait_recv()
        k = link_half(link, True)
        fill(near_out.at[link], cum_m, 3, links[link], k, (sib_in.at[1 + link], k * half))
        beside_copy(link, 0).start()
    chain_far(0, 1)
    for link in range(2):
        diag(1 - link).wait_recv()
        k = link_half(link, False)
        fill(
            near_out.at[link], cum_m, 3, links[link], k,
            (sib_in.at[1 + link], k * half), (diag_in.at[1 - link], 0),
        )
        beside_copy(link, 1).start()
    chain_end(0)
    chain_far(1, 0)
    chain_end(1)
    to_sib(3).wait_recv()

    def blocks(body, a, b):
        def step(p, _):
            body(p, pl.ds(pl.multiple_of(p * tile, tile), tile))
            return 0

        lax.fori_loop(a, b, step, 0, unroll=8)

    def base(p, at):
        o_ref[:, at] = (
            cum_f[table[1, c * per_slab + p]] + cum_m[table[3, r * per_slab + p]]
            + sib_in[3, p].astype(f32)
        )

    def add(k, *sources):
        def body(p, at):
            out = o_ref[:, at]
            for source in sources:
                out = out + source[p].astype(f32)
            o_ref[:, at] = out

        blocks(body, k * half, (k + 1) * half)

    blocks(base, 0, per_slab)

    @pl.when(end)
    def _():
        for k in range(2):
            to_end(k).wait_recv()
            add(k, z_in.at[0])

    chain_far(1, 1)
    for link in range(2):
        beside_copy(link, 0).wait_recv()
        add(link_half(link, True), near_in.at[link])
    for link in range(2):
        beside_copy(link, 1).wait_recv()
        add(link_half(link, False), near_in.at[link])

    @pl.when(mid)
    def _():
        for k in range(2):
            far(1, k).wait_recv()
            near(2, k).wait_recv()
            add(k, z_in.at[4], z_in.at[2])

    for k in range(2):

        @pl.when(c < 3)
        def _():
            z_copy(0, c, k, c + 1).wait_send()

        @pl.when(c > 0)
        def _():
            z_copy(1, c, k, c - 1).wait_send()

        @pl.when(mid)
        def _():
            z_copy(2, c - 1, k, c + 1).wait_send()
            z_copy(3, c + 1, k, c - 1).wait_send()
            z_copy(4, far_end, k, near_end).wait_send()

        for i in range(3):
            near(i, k).wait_send()
        for link in range(2):
            own_copy(link, r, k).wait_send()
            beside_copy(link, k).wait_send()
        for i, owner in enumerate((r, xn, yn, dn)):
            sib_copy(i, xc.at[owner, part(k)], owner, k).wait_send()
    for link in range(2):
        pass_copy(link, links[1 - link]).wait_send()
        diag(link).wait_send()
    for j in range(4):
        to_sib(j).wait_send()


def fused(tiles, tile_coords, tile_counts, x):
    slots, tile = tiles.shape[2], tiles.shape[-1]
    vecs, width = x.shape
    slab = width // tile
    half = slab // 2
    dma, bf16, f32, i32 = pltpu.SemaphoreType.DMA, jnp.bfloat16, jnp.float32, jnp.int32

    def blocks(*lead, dtype=bf16):
        return pltpu.VMEM((*lead, vecs, tile), dtype)

    return pl.pallas_call(
        fused_kernel,
        out_shape=jax.ShapeDtypeStruct(x.shape, f32),
        in_specs=[pl.BlockSpec(memory_space=pltpu.HBM)] * 4,
        out_specs=pl.BlockSpec(memory_space=pltpu.VMEM),
        scratch_shapes=[
            pltpu.VMEM(x.shape, bf16),
            blocks(4, slab),
            blocks(8, slab),
            pltpu.VMEM((slots, tile, tile), bf16),
            pltpu.VMEM((slots, tile, tile), bf16),
            pltpu.VMEM((2, tile, tile), bf16),
            blocks(slots, dtype=f32),
            blocks(slots + 1, dtype=f32),
            blocks(slots + 1, dtype=f32),
            pltpu.VMEM((8, 8 * slab), i32),
            blocks(3, slab),
            blocks(5, slab),
            blocks(4, slab),
            blocks(4, slab),
            blocks(2, half),
            blocks(2, half),
            blocks(2, slab),
            blocks(2, slab),
            pltpu.SMEM(tile_coords.shape, i32),
            pltpu.VMEM(tile_coords.shape, i32),
            pltpu.VMEM((1, 1), i32),
            pltpu.SMEM((8, 8 * slab), i32),
            dma((5,)),
            dma((slots // GROUP,)),
            dma((5, 2)), dma((4, 2)),
            dma((2, 3)), dma((2, 3)),
            dma((4, 2)), dma((4, 2)),
            dma((3, 2)), dma((5, 2)),
            dma((4,)), dma((4,)),
            dma((2,)), dma((2,)),
            dma((2, 2)), dma((2, 2)),
        ],
        compiler_params=pltpu.CompilerParams(
            collective_id=0, has_side_effects=True, vmem_limit_bytes=VMEM_LIMIT
        ),
        name="fused_product",
    )(tile_coords, tile_counts, x, tiles)


def apply_kernel(
    slots, tile, per_slab, n_cols, coords, count,
    t_ref, xr_ref, xc_ref, f_ref, m_ref, facc, macc,
):
    step = pl.program_id(0)
    group = t_ref.shape[2]

    @pl.when(step == 0)
    def _():
        facc[...] = jnp.zeros_like(facc)
        macc[...] = jnp.zeros_like(macc)

    def place(s):
        tile_row, tile_col = coords[s], coords[slots + s]
        local = tile_row % (per_slab * n_cols)
        row_at = (local // per_slab, pl.multiple_of(local % per_slab * tile, tile))
        col_at = (
            tile_col // (per_slab * n_cols), pl.multiple_of(tile_col % per_slab * tile, tile),
        )
        return row_at, col_at

    def run(masked):
        made = []
        for g in range(group):
            s = step * group + g
            (ro, rp), (co, cp) = place(s)
            x_row = xr_ref[ro, :, pl.ds(rp, tile)]
            x_col = xc_ref[co, :, pl.ds(cp, tile)]
            upper = lower = t_ref[0, 0, g]
            if masked:
                off = coords[s] != coords[slots + s]
                down = lax.broadcasted_iota(jnp.int32, (tile, tile), 0)
                down = jnp.where(off, -1, down)
                across = lax.broadcasted_iota(jnp.int32, (tile, tile), 1)
                stored = upper.astype(jnp.float32)
                upper = jnp.where(down <= across, stored, 0.0).astype(jnp.bfloat16)
                lower = jnp.where(down < across, stored, 0.0).astype(jnp.bfloat16)
            forward = lax.dot_general(
                x_col, upper, (((1,), (1,)), ((), ())), preferred_element_type=jnp.float32
            )
            mirror = lax.dot_general(
                x_row, lower, (((1,), (0,)), ((), ())), preferred_element_type=jnp.float32
            )
            if masked:
                live = s < count[0]
                forward = jnp.where(live, forward, 0.0)
                mirror = jnp.where(live, mirror, 0.0)
            made.append((forward, mirror))
        for g in range(group):
            (ro, rp), (co, cp) = place(step * group + g)
            forward, mirror = made[g]
            facc[ro, :, pl.ds(rp, tile)] += forward
            macc[co, :, pl.ds(cp, tile)] += mirror

    special = coords[step * group] == coords[slots + step * group]
    for g in range(1, group):
        s = step * group + g
        special = special | (coords[s] == coords[slots + s])
    special = special | (step * group + group > count[0])

    @pl.when(special)
    def _():
        run(True)

    @pl.when(jnp.logical_not(special))
    def _():
        run(False)

    @pl.when(step == pl.num_programs(0) - 1)
    def _():
        f_ref[...] = facc[...].astype(f_ref.dtype)
        m_ref[...] = macc[...].astype(m_ref.dtype)


def apply_tiles(tiles, coords, count, xr, xc, tile):
    slots = tiles.shape[2]
    group = GROUP if slots % GROUP == 0 else 1
    n_cols = xr.shape[0]
    per_slab = xr.shape[2] // tile
    whole = lambda a: pl.BlockSpec(a.shape, lambda i, *_: (0, 0, 0))
    return pl.pallas_call(
        functools.partial(apply_kernel, slots, tile, per_slab, n_cols),
        out_shape=(
            jax.ShapeDtypeStruct(xr.shape, jnp.bfloat16),
            jax.ShapeDtypeStruct(xc.shape, jnp.bfloat16),
        ),
        grid_spec=pltpu.PrefetchScalarGridSpec(
            num_scalar_prefetch=2,
            grid=(slots // group,),
            in_specs=[
                pl.BlockSpec((1, 1, group, tile, tile), lambda i, *_: (0, 0, i, 0, 0)),
                whole(xr),
                whole(xc),
            ],
            out_specs=(whole(xr), whole(xc)),
            scratch_shapes=[
                pltpu.VMEM(xr.shape, jnp.float32),
                pltpu.VMEM(xc.shape, jnp.float32),
            ],
        ),
        compiler_params=pltpu.CompilerParams(vmem_limit_bytes=VMEM_LIMIT),
        name="apply_tiles",
    )(coords, count, tiles, xr, xc)


def shards(n_rows, n_cols, tiles, tile_coords, tile_counts, vectors):
    tile = tiles.shape[-1]
    x = vectors.T
    if (n_rows, n_cols) == (8, 4):
        return fused(tiles, tile_coords, tile_counts, x).T
    coords, count = tile_coords.reshape(-1), tile_counts.reshape(-1)
    xr = lax.all_gather(x, "col", axis=0)
    xc = lax.all_gather(x, "row", axis=0)
    f, m = apply_tiles(tiles, coords, count, xr, xc, tile)
    f = lax.all_to_all(f, "col", 0, 0, tiled=True)
    m = lax.all_to_all(m, "row", 0, 0, tiled=True)
    return (jnp.sum(f.astype(jnp.float32), 0) + jnp.sum(m.astype(jnp.float32), 0)).T


def solution(mesh):
    in_specs = (
        P("row", "col", None, None, None),
        P(None, "row", "col", None),
        P("row", "col"),
        P(("row", "col"), None),
    )
    out_specs = P(("row", "col"), None)
    body = functools.partial(shards, mesh.shape["row"], mesh.shape["col"])
    return jax.shard_map(body, mesh=mesh, in_specs=in_specs, out_specs=out_specs, check_vma=False)
```

```python
import functools

import jax
import jax.numpy as jnp
from jax import lax
from jax.experimental import pallas as pl
from jax.experimental.pallas import tpu as pltpu
from jax.sharding import PartitionSpec as P

MESH = pl.DeviceIdType.MESH
VMEM_LIMIT = 48 * 1024 * 1024
GROUP = 8
LAG = 8
LATE_ROWS = 35
LATE_COLS = 28


def fused_kernel(
    coords_hbm, count_hbm, x_hbm, t_ref, o_ref,
    xv, xr, xc, xr_late, xc_late, upper, lower, tri, made, cum_f, cum_m, table_v,
    z_out, z_in, sib_out, sib_in, diag_out, diag_in, near_out, near_in,
    coords, coords_v, count_v, table,
    in_sem, tile_sem, zs, zr, ys, yr, ss, sr, ps, pr, bs, br, ds, dr, ns, nr,
):
    r, c = lax.axis_index("row"), lax.axis_index("col")
    chip, core = r // 2, r % 2
    cx, cy = chip % 2, chip // 2
    beside, across, opposite = 2 * cy + 1 - cx, 2 * (1 - cy) + cx, 3 - chip
    sib = 2 * chip + 1 - core
    xn, yn, dn = 2 * beside + core, 2 * across + core, 2 * opposite + core
    mid = (c == 1) | (c == 2)
    end = (c == 0) | (c == 3)
    next_mid = 1 + c // 3
    near_end, far_mid = 3 * (c - 1), 3 - c
    far_end = 3 - near_end
    slots, tile = upper.shape[0], upper.shape[1]
    vecs = x_hbm.shape[0]
    per_slab = x_hbm.shape[1] // tile
    half = per_slab // 2
    groups = slots // GROUP
    span = 4 * per_slab
    f32, bf16, i32 = jnp.float32, jnp.bfloat16, jnp.int32

    late_row = jnp.where(c < 2, 3, 0)
    late_col = 2 * opposite + 1 - core

    def part(k):
        return pl.ds(k * half, half)

    x_copy = pltpu.make_async_copy(x_hbm, xv, in_sem.at[0])
    coords_copy = pltpu.make_async_copy(coords_hbm, coords, in_sem.at[1])
    coords_v_copy = pltpu.make_async_copy(coords_hbm, coords_v, in_sem.at[2])
    count_copy = pltpu.make_async_copy(count_hbm, count_v, in_sem.at[3])
    table_copy = pltpu.make_async_copy(table_v, table, in_sem.at[4])
    for copy in (x_copy, coords_v_copy, count_copy, coords_copy):
        copy.start()

    def tile_copy(g):
        at = pl.ds(g * GROUP, GROUP)
        return pltpu.make_async_copy(t_ref.at[0, 0, at], lower.at[at], tile_sem.at[g])

    barrier = pltpu.get_barrier_semaphore()
    for row in (xn, yn, sib):
        pl.semaphore_signal(barrier, inc=1, device_id=(row, c), device_id_type=MESH)

    @pl.when(c > 0)
    def _():
        pl.semaphore_signal(barrier, inc=1, device_id=(r, c - 1), device_id_type=MESH)

    @pl.when(c < 3)
    def _():
        pl.semaphore_signal(barrier, inc=1, device_id=(r, c + 1), device_id_type=MESH)

    def start_tiles(g, _):
        tile_copy(g).start()
        return 0

    x_copy.wait()
    lax.fori_loop(0, groups, start_tiles, 0)
    for p in range(per_slab):
        xr[c, p] = xv[:, p * tile : (p + 1) * tile]

    @pl.when(mid)
    def _():
        pl.semaphore_wait(barrier, 5)

    @pl.when(end)
    def _():
        pl.semaphore_wait(barrier, 4)

    def remote(src, dst, send, recv, row, col):
        return pltpu.make_async_remote_copy(
            src, dst, send, recv, device_id=(row, col), device_id_type=MESH
        )

    def z_copy(j, owner, k, to, src=None, dst=None):
        src = xr.at[owner, part(k)] if src is None else src.at[part(k)]
        dst = xr.at[owner, part(k)] if dst is None else dst.at[part(k)]
        return remote(src, dst, zs.at[j, k], zr.at[owner, k], r, to)

    def z_inner(k):
        return z_copy(2, near_end, k, far_mid, dst=xr_late)

    def z_outer(k):
        return z_copy(3, far_mid, k, near_end)

    def z_far(k):
        return z_copy(4, far_end, k, near_end, src=xr_late, dst=xr_late)

    def link_half(link, first):
        return (0 if first else 1) if link == 0 else (1 if first else 0)

    links = (xn, yn)

    def own_copy(link, owner, i):
        k = link_half(link, i == 0)
        return remote(
            xr.at[c, part(k)], xc.at[owner, part(k)], ys.at[link, i], yr.at[link, i],
            links[link], c,
        )

    def pass_copy(link, owner):
        k = link_half(link, False)
        block = xc.at[owner, part(k)]
        return remote(block, block, ys.at[link, 2], yr.at[link, 2], links[link], c)

    def sib_copy(i, src, owner, k):
        dst = xc_late.at[part(k)] if i == 3 else xc.at[owner, part(k)]
        return remote(src, dst, ss.at[i, k], sr.at[i, k], sib, c)

    def start_own(k):
        @pl.when(c < 3)
        def _():
            z_copy(0, c, k, c + 1).start()

        @pl.when(c > 0)
        def _():
            z_copy(1, c, k, c - 1).start()

        for link in range(2):
            own_copy(link, r, k).start()

    start_own(0)
    start_own(1)
    for k in range(2):
        sib_copy(0, xr.at[c, part(k)], r, k).start()
    for p in range(per_slab):
        xc[r, p] = xv[:, p * tile : (p + 1) * tile]

    coords_v_copy.wait()
    count_copy.wait()
    rows_v, cols_v = coords_v[0, 0], coords_v[1, 0]
    lane = lax.broadcasted_iota(i32, (slots, slots), 1)
    down = lax.broadcasted_iota(i32, (slots, slots), 0)
    live = lax.broadcasted_iota(i32, (1, slots), 1) < count_v[0:1, 0:1]
    places = (rows_v % span, cols_v // span * per_slab + cols_v % per_slab)
    width = table_v.shape[1]
    order = lax.broadcasted_iota(i32, (slots, width), 0) + 1
    target = lax.broadcasted_iota(i32, (slots, width), 1)
    lates = (cols_v // span == late_col, rows_v % span // per_slab == late_row)

    def on_rows(values):
        wide = jnp.where(down == lane, jnp.broadcast_to(values, (slots, slots)), 0)
        return jnp.sum(wide.astype(f32), axis=1, keepdims=True).astype(i32)

    def count_of(mask):
        return jnp.sum(jnp.where(mask, 1.0, 0.0), axis=1, keepdims=True).astype(i32)

    for k in range(2):
        place = jnp.where(live, places[k], -1)
        late = jnp.where(live & lates[k], 1, 0)
        ahead = count_of((late == 0) & (lane < down))
        behind = count_of((late == 1) & (lane >= down))
        spot = jnp.where(on_rows(late) == 1, slots - behind, ahead)
        here = spot == lane
        table_v[4 + k : 5 + k, 0:slots] = jnp.max(
            jnp.where(here, down, 0), axis=0, keepdims=True
        )
        place = jnp.max(jnp.where(here, on_rows(place) + 1, 0), axis=0, keepdims=True) - 1
        tall = on_rows(place)
        before = jnp.where((tall == place) & (down < lane), down + 1, 0)
        table_v[2 * k : 2 * k + 1, 0:slots] = jnp.max(before, axis=0, keepdims=True)
        found = jnp.where(tall == target, order, 0)
        table_v[2 * k + 1 : 2 * k + 2, :] = jnp.max(found, axis=0, keepdims=True)
    table_copy.start()
    cum_f[0] = jnp.zeros(cum_f.shape[1:], f32)
    cum_m[0] = jnp.zeros(cum_m.shape[1:], f32)

    down = lax.broadcasted_iota(i32, (tile, tile), 0)
    over = lax.broadcasted_iota(i32, (tile, tile), 1)
    def clear_late(p, _):
        xr[late_row, p] = jnp.zeros(xr.shape[2:], bf16)
        xc[late_col, p] = jnp.zeros(xc.shape[2:], bf16)
        return 0

    lax.fori_loop(0, per_slab, clear_late, 0)
    tri[0] = (down >= over).astype(f32).astype(bf16)
    tri[1] = (down < over).astype(f32).astype(bf16)
    coords_copy.wait()

    def split_group(g, _):
        tile_copy(g).wait()
        for i in range(GROUP):
            s = g * GROUP + i
            gap = jnp.full((1, tile), coords[0, 0, 0, s] - coords[1, 0, 0, s], i32)
            off = jnp.minimum(gap * gap, 1).astype(f32).astype(bf16)
            stored = lower[s]
            upper[s] = stored.T * jnp.maximum(tri[0], off)
            lower[s] = stored * jnp.maximum(tri[1], off)
        return 0

    def split(a, b):
        lax.fori_loop(a * groups // 10, b * groups // 10, split_group, 0)

    def z_pass_one(k):
        @pl.when(mid)
        def _():
            z_copy(2, near_end, k, far_mid).wait_recv()
            z_inner(k).start()
            z_outer(k).wait_recv()
            z_outer(k).start()

    def z_pass_two(k):
        @pl.when(mid)
        def _():
            z_far(k).wait_recv()
            z_far(k).start()

    split(0, 2)
    for link in range(2):
        own_copy(link, links[link], 0).wait_recv()
        pass_copy(1 - link, links[link]).start()
        k = link_half(link, True)
        sib_copy(1 + link, xc.at[links[link], part(k)], links[link], k).start()
    z_pass_one(0)
    split(2, 5)
    for link in range(2):
        own_copy(link, links[link], 1).wait_recv()
        k = link_half(link, False)
        sib_copy(1 + link, xc.at[links[link], part(k)], links[link], k).start()
    z_pass_one(1)
    split(5, 8)
    z_pass_two(0)
    split(8, 10)
    for link in range(2):
        pass_copy(link, dn).wait_recv()
        k = link_half(link, False)
        sib_copy(3, xc.at[dn, part(k)], dn, k).start()
    z_pass_two(1)
    table_copy.wait()

    def sib_wait(i, owner):
        for k in range(2):
            sib_copy(i, xc.at[owner, part(k)], owner, k).wait_recv()

    for i, owner in enumerate((sib, 2 * beside + 1 - core, 2 * across + 1 - core)):
        sib_wait(i, owner)

    def fetch_late(dst, owner, src):
        def body(p, _):
            dst[owner, p] = src[p]
            return 0

        lax.fori_loop(0, per_slab, body, 0, unroll=8)

    def running_sums(make, cum, at, a, b):
        def link(n):
            cum[n + 1] = made[n] + cum[table[at, n]]

        for n in range(a, b):
            make(n)
            if n - LAG >= a:
                link(n - LAG)
        for n in range(max(a, b - LAG), b):
            link(n)

    def forward(n):
        s = table[4, n]
        col = coords[1, 0, 0, s]
        made[n] = jnp.dot(
            xc[lax.div(col, span), lax.rem(col, per_slab)], upper[s],
            preferred_element_type=f32,
        )

    def mirror(n):
        s = table[5, n]
        row = lax.rem(coords[0, 0, 0, s], span)
        made[n] = jnp.dot(
            xr[lax.div(row, per_slab), lax.rem(row, per_slab)], lower[s],
            preferred_element_type=f32,
        )

    def fill(dst, cum, at, owner, k, *more, to=None):
        base = k * half

        def body(i, _):
            out = cum[table[at, owner * per_slab + base + i]]
            for source, offset in more:
                out = out + source[offset + i].astype(f32)
            dst[(base if to is None else to) + i] = out.astype(dst.dtype)
            return 0

        lax.fori_loop(0, half, body, 0, unroll=8)

    def near(i, k):
        return remote(
            z_out.at[i, part(k)], z_in.at[i, part(k)], ps.at[i, k], pr.at[i, k], r, next_mid
        )

    def far(i, k):
        return remote(
            z_out.at[i, part(k)], z_in.at[3 + i, part(k)], ps.at[i, k], pr.at[3 + i, k],
            r, far_mid,
        )

    def to_end(k):
        return remote(
            z_out.at[2, part(k)], z_in.at[0, part(k)], ps.at[2, k], pr.at[0, k], r, near_end
        )

    def chain_far(i, k):
        @pl.when(mid)
        def _():
            near(i, k).wait_recv()
            owner = far_end if i == 0 else far_mid
            fill(z_out.at[i], cum_f, 1, owner, k, (z_in.at[i], k * half))
            far(i, k).start()

    def chain_end(k):
        @pl.when(mid)
        def _():
            far(0, k).wait_recv()
            fill(z_out.at[2], cum_f, 1, near_end, k, (z_in.at[3], k * half))
            to_end(k).start()

    def to_sib(j):
        return remote(sib_out.at[j], sib_in.at[j], bs.at[j], br.at[j], sib, c)

    def diag(link):
        return remote(
            diag_out.at[link], diag_in.at[link], ds.at[link], dr.at[link], links[link], c
        )

    def beside_copy(link, i):
        k = link_half(link, i == 0)
        return remote(
            near_out.at[link, part(k)], near_in.at[link, part(k)],
            ns.at[link, i], nr.at[link, i], links[link], c,
        )

    running_sums(forward, cum_f, 0, 0, slots - LATE_COLS)
    sib_wait(3, late_col)
    fetch_late(xc, late_col, xc_late)
    running_sums(forward, cum_f, 0, slots - LATE_COLS, slots)

    @pl.when(end)
    def _():
        for i, owner in enumerate((3 - c, 3 - next_mid, next_mid)):
            for k in range(2):
                fill(z_out.at[i], cum_f, 1, owner, k)
                near(i, k).start()

    @pl.when(end)
    def _():
        for owner in (next_mid, 3 - next_mid):
            for k in range(2):
                z_copy(0, owner, k, next_mid).wait_recv()

    running_sums(mirror, cum_m, 2, 0, slots - LATE_ROWS)

    @pl.when(end)
    def _():
        for k in range(2):
            z_copy(0, late_row, k, next_mid, dst=xr_late).wait_recv()

    fetch_late(xr, late_row, xr_late)
    running_sums(mirror, cum_m, 2, slots - LATE_ROWS, slots)
    for j, to in enumerate((opposite, beside, across, chip)):
        for k in range(2):
            fill(sib_out.at[j], cum_m, 3, 2 * to + 1 - core, k)
        to_sib(j).start()
    chain_far(0, 0)
    to_sib(0).wait_recv()
    for link in range(2):
        fill(diag_out.at[link], cum_m, 3, dn, link, (sib_in.at[0], link * half), to=0)
        diag(link).start()
    for link in range(2):
        to_sib(1 + link).wait_recv()
        k = link_half(link, True)
        fill(near_out.at[link], cum_m, 3, links[link], k, (sib_in.at[1 + link], k * half))
        beside_copy(link, 0).start()
    chain_far(0, 1)
    for link in range(2):
        diag(1 - link).wait_recv()
        k = link_half(link, False)
        fill(
            near_out.at[link], cum_m, 3, links[link], k,
            (sib_in.at[1 + link], k * half), (diag_in.at[1 - link], 0),
        )
        beside_copy(link, 1).start()
    chain_end(0)
    chain_far(1, 0)
    chain_end(1)
    to_sib(3).wait_recv()

    def blocks(body, a, b):
        def step(p, _):
            body(p, pl.ds(pl.multiple_of(p * tile, tile), tile))
            return 0

        lax.fori_loop(a, b, step, 0, unroll=8)

    def base(p, at):
        o_ref[:, at] = (
            cum_f[table[1, c * per_slab + p]] + cum_m[table[3, r * per_slab + p]]
            + sib_in[3, p].astype(f32)
        )

    def add(k, *sources):
        def body(p, at):
            out = o_ref[:, at]
            for source in sources:
                out = out + source[p].astype(f32)
            o_ref[:, at] = out

        blocks(body, k * half, (k + 1) * half)

    blocks(base, 0, per_slab)

    @pl.when(end)
    def _():
        for k in range(2):
            to_end(k).wait_recv()
            add(k, z_in.at[0])

    chain_far(1, 1)
    for link in range(2):
        beside_copy(link, 0).wait_recv()
        add(link_half(link, True), near_in.at[link])
    for link in range(2):
        beside_copy(link, 1).wait_recv()
        add(link_half(link, False), near_in.at[link])

    @pl.when(mid)
    def _():
        for k in range(2):
            far(1, k).wait_recv()
            near(2, k).wait_recv()
            add(k, z_in.at[4], z_in.at[2])

    for k in range(2):

        @pl.when(c < 3)
        def _():
            z_copy(0, c, k, c + 1).wait_send()

        @pl.when(c > 0)
        def _():
            z_copy(1, c, k, c - 1).wait_send()

        @pl.when(mid)
        def _():
            z_inner(k).wait_send()
            z_outer(k).wait_send()
            z_far(k).wait_send()

        for i in range(3):
            near(i, k).wait_send()
        for link in range(2):
            own_copy(link, r, k).wait_send()
            beside_copy(link, k).wait_send()
        for i, owner in enumerate((r, xn, yn, dn)):
            sib_copy(i, xc.at[owner, part(k)], owner, k).wait_send()
    for link in range(2):
        pass_copy(link, links[1 - link]).wait_send()
        diag(link).wait_send()
    for j in range(4):
        to_sib(j).wait_send()


def fused(tiles, tile_coords, tile_counts, x):
    slots, tile = tiles.shape[2], tiles.shape[-1]
    vecs, width = x.shape
    slab = width // tile
    half = slab // 2
    dma, bf16, f32, i32 = pltpu.SemaphoreType.DMA, jnp.bfloat16, jnp.float32, jnp.int32

    def blocks(*lead, dtype=bf16):
        return pltpu.VMEM((*lead, vecs, tile), dtype)

    return pl.pallas_call(
        fused_kernel,
        out_shape=jax.ShapeDtypeStruct(x.shape, f32),
        in_specs=[pl.BlockSpec(memory_space=pltpu.HBM)] * 4,
        out_specs=pl.BlockSpec(memory_space=pltpu.VMEM),
        scratch_shapes=[
            pltpu.VMEM(x.shape, bf16),
            blocks(4, slab),
            blocks(8, slab),
            blocks(slab),
            blocks(slab),
            pltpu.VMEM((slots, tile, tile), bf16),
            pltpu.VMEM((slots, tile, tile), bf16),
            pltpu.VMEM((2, tile, tile), bf16),
            blocks(slots, dtype=f32),
            blocks(slots + 1, dtype=f32),
            blocks(slots + 1, dtype=f32),
            pltpu.VMEM((8, 8 * slab), i32),
            blocks(3, slab),
            blocks(5, slab),
            blocks(4, slab),
            blocks(4, slab),
            blocks(2, half),
            blocks(2, half),
            blocks(2, slab),
            blocks(2, slab),
            pltpu.SMEM(tile_coords.shape, i32),
            pltpu.VMEM(tile_coords.shape, i32),
            pltpu.VMEM((1, 1), i32),
            pltpu.SMEM((8, 8 * slab), i32),
            dma((5,)),
            dma((slots // GROUP,)),
            dma((5, 2)), dma((4, 2)),
            dma((2, 3)), dma((2, 3)),
            dma((4, 2)), dma((4, 2)),
            dma((3, 2)), dma((5, 2)),
            dma((4,)), dma((4,)),
            dma((2,)), dma((2,)),
            dma((2, 2)), dma((2, 2)),
        ],
        compiler_params=pltpu.CompilerParams(
            collective_id=0, has_side_effects=True, vmem_limit_bytes=VMEM_LIMIT
        ),
        name="fused_product",
    )(
        pltpu.with_memory_space_constraint(tile_coords, pltpu.HBM), tile_counts,
        pltpu.with_memory_space_constraint(x, pltpu.HBM), tiles,
    )


def apply_kernel(
    slots, tile, per_slab, n_cols, coords, count,
    t_ref, xr_ref, xc_ref, f_ref, m_ref, facc, macc,
):
    step = pl.program_id(0)
    group = t_ref.shape[2]

    @pl.when(step == 0)
    def _():
        facc[...] = jnp.zeros_like(facc)
        macc[...] = jnp.zeros_like(macc)

    def place(s):
        tile_row, tile_col = coords[s], coords[slots + s]
        local = tile_row % (per_slab * n_cols)
        row_at = (local // per_slab, pl.multiple_of(local % per_slab * tile, tile))
        col_at = (
            tile_col // (per_slab * n_cols), pl.multiple_of(tile_col % per_slab * tile, tile),
        )
        return row_at, col_at

    def run(masked):
        made = []
        for g in range(group):
            s = step * group + g
            (ro, rp), (co, cp) = place(s)
            x_row = xr_ref[ro, :, pl.ds(rp, tile)]
            x_col = xc_ref[co, :, pl.ds(cp, tile)]
            upper = lower = t_ref[0, 0, g]
            if masked:
                off = coords[s] != coords[slots + s]
                down = lax.broadcasted_iota(jnp.int32, (tile, tile), 0)
                down = jnp.where(off, -1, down)
                across = lax.broadcasted_iota(jnp.int32, (tile, tile), 1)
                stored = upper.astype(jnp.float32)
                upper = jnp.where(down <= across, stored, 0.0).astype(jnp.bfloat16)
                lower = jnp.where(down < across, stored, 0.0).astype(jnp.bfloat16)
            forward = lax.dot_general(
                x_col, upper, (((1,), (1,)), ((), ())), preferred_element_type=jnp.float32
            )
            mirror = lax.dot_general(
                x_row, lower, (((1,), (0,)), ((), ())), preferred_element_type=jnp.float32
            )
            if masked:
                live = s < count[0]
                forward = jnp.where(live, forward, 0.0)
                mirror = jnp.where(live, mirror, 0.0)
            made.append((forward, mirror))
        for g in range(group):
            (ro, rp), (co, cp) = place(step * group + g)
            forward, mirror = made[g]
            facc[ro, :, pl.ds(rp, tile)] += forward
            macc[co, :, pl.ds(cp, tile)] += mirror

    special = coords[step * group] == coords[slots + step * group]
    for g in range(1, group):
        s = step * group + g
        special = special | (coords[s] == coords[slots + s])
    special = special | (step * group + group > count[0])

    @pl.when(special)
    def _():
        run(True)

    @pl.when(jnp.logical_not(special))
    def _():
        run(False)

    @pl.when(step == pl.num_programs(0) - 1)
    def _():
        f_ref[...] = facc[...].astype(f_ref.dtype)
        m_ref[...] = macc[...].astype(m_ref.dtype)


def apply_tiles(tiles, coords, count, xr, xc, tile):
    slots = tiles.shape[2]
    group = GROUP if slots % GROUP == 0 else 1
    n_cols = xr.shape[0]
    per_slab = xr.shape[2] // tile
    whole = lambda a: pl.BlockSpec(a.shape, lambda i, *_: (0, 0, 0))
    return pl.pallas_call(
        functools.partial(apply_kernel, slots, tile, per_slab, n_cols),
        out_shape=(
            jax.ShapeDtypeStruct(xr.shape, jnp.bfloat16),
            jax.ShapeDtypeStruct(xc.shape, jnp.bfloat16),
        ),
        grid_spec=pltpu.PrefetchScalarGridSpec(
            num_scalar_prefetch=2,
            grid=(slots // group,),
            in_specs=[
                pl.BlockSpec((1, 1, group, tile, tile), lambda i, *_: (0, 0, i, 0, 0)),
                whole(xr),
                whole(xc),
            ],
            out_specs=(whole(xr), whole(xc)),
            scratch_shapes=[
                pltpu.VMEM(xr.shape, jnp.float32),
                pltpu.VMEM(xc.shape, jnp.float32),
            ],
        ),
        compiler_params=pltpu.CompilerParams(vmem_limit_bytes=VMEM_LIMIT),
        name="apply_tiles",
    )(coords, count, tiles, xr, xc)


def shards(n_rows, n_cols, tiles, tile_coords, tile_counts, vectors):
    tile = tiles.shape[-1]
    x = vectors.T
    if (n_rows, n_cols) == (8, 4):
        return fused(tiles, tile_coords, tile_counts, x).T
    coords, count = tile_coords.reshape(-1), tile_counts.reshape(-1)
    xr = lax.all_gather(x, "col", axis=0)
    xc = lax.all_gather(x, "row", axis=0)
    f, m = apply_tiles(tiles, coords, count, xr, xc, tile)
    f = lax.all_to_all(f, "col", 0, 0, tiled=True)
    m = lax.all_to_all(m, "row", 0, 0, tiled=True)
    return (jnp.sum(f.astype(jnp.float32), 0) + jnp.sum(m.astype(jnp.float32), 0)).T


def solution(mesh):
    in_specs = (
        P("row", "col", None, None, None),
        P(None, "row", "col", None),
        P("row", "col"),
        P(("row", "col"), None),
    )
    out_specs = P(("row", "col"), None)
    body = functools.partial(shards, mesh.shape["row"], mesh.shape["col"])
    return jax.shard_map(body, mesh=mesh, in_specs=in_specs, out_specs=out_specs, check_vma=False)
```

```python
import functools

import jax
import jax.numpy as jnp
from jax import lax
from jax.experimental import pallas as pl
from jax.experimental.pallas import tpu as pltpu
from jax.sharding import PartitionSpec as P

MESH = pl.DeviceIdType.MESH
VMEM_LIMIT = 48 * 1024 * 1024
GROUP = 8
LAG = 8
LATE_ROWS = 35
LATE_COLS = 28


def fused_kernel(
    coords_hbm, count_hbm, x_hbm, t_ref, o_ref,
    xv, xr, xc, xr_late, xc_late, upper, lower, tri, made, made_m, cum_f, cum_m, table_v,
    z_out, z_in, sib_out, sib_in, diag_out, diag_in, near_out, near_in,
    coords, coords_v, count_v, table,
    in_sem, tile_sem, zs, zr, ys, yr, ss, sr, ps, pr, bs, br, ds, dr, ns, nr,
):
    r, c = lax.axis_index("row"), lax.axis_index("col")
    chip, core = r // 2, r % 2
    cx, cy = chip % 2, chip // 2
    beside, across, opposite = 2 * cy + 1 - cx, 2 * (1 - cy) + cx, 3 - chip
    sib = 2 * chip + 1 - core
    xn, yn, dn = 2 * beside + core, 2 * across + core, 2 * opposite + core
    mid = (c == 1) | (c == 2)
    end = (c == 0) | (c == 3)
    next_mid = 1 + c // 3
    near_end, far_mid = 3 * (c - 1), 3 - c
    far_end = 3 - near_end
    slots, tile = upper.shape[0], upper.shape[1]
    vecs = x_hbm.shape[0]
    per_slab = x_hbm.shape[1] // tile
    half = per_slab // 2
    pairs, some = per_slab // 2, vecs // 2
    quarter = pairs // 2
    groups = slots // GROUP
    span = 4 * per_slab
    f32, bf16, i32 = jnp.float32, jnp.bfloat16, jnp.int32

    late_row = jnp.where(c < 2, 3, 0)
    late_col = 2 * opposite + 1 - core

    def part(k):
        return pl.ds(k * half, half)

    x_copy = pltpu.make_async_copy(x_hbm, xv, in_sem.at[0])
    coords_copy = pltpu.make_async_copy(coords_hbm, coords, in_sem.at[1])
    coords_v_copy = pltpu.make_async_copy(coords_hbm, coords_v, in_sem.at[2])
    count_copy = pltpu.make_async_copy(count_hbm, count_v, in_sem.at[3])
    table_copy = pltpu.make_async_copy(table_v, table, in_sem.at[4])
    for copy in (x_copy, coords_v_copy, count_copy, coords_copy):
        copy.start()

    def tile_copy(g):
        at = pl.ds(g * GROUP, GROUP)
        return pltpu.make_async_copy(t_ref.at[0, 0, at], lower.at[at], tile_sem.at[g])

    barrier = pltpu.get_barrier_semaphore()
    for row in (xn, yn, sib):
        pl.semaphore_signal(barrier, inc=1, device_id=(row, c), device_id_type=MESH)

    @pl.when(c > 0)
    def _():
        pl.semaphore_signal(barrier, inc=1, device_id=(r, c - 1), device_id_type=MESH)

    @pl.when(c < 3)
    def _():
        pl.semaphore_signal(barrier, inc=1, device_id=(r, c + 1), device_id_type=MESH)

    def start_tiles(g, _):
        tile_copy(g).start()
        return 0

    x_copy.wait()
    for p in range(per_slab):
        xc[r, p] = xv[:, p * tile : (p + 1) * tile]
    @pl.when(mid)
    def _():
        pl.semaphore_wait(barrier, 5)

    @pl.when(end)
    def _():
        pl.semaphore_wait(barrier, 4)

    def remote(src, dst, send, recv, row, col):
        return pltpu.make_async_remote_copy(
            src, dst, send, recv, device_id=(row, col), device_id_type=MESH
        )

    def z_copy(j, owner, h, to, src=None, dst=None):
        src = xr.at[h, owner] if src is None else src.at[h]
        dst = xr.at[h, owner] if dst is None else dst.at[h]
        return remote(src, dst, zs.at[j, h], zr.at[owner, h], r, to)

    def z_inner(k):
        return z_copy(2, near_end, k, far_mid, dst=xr_late)

    def z_outer(k):
        return z_copy(3, far_mid, k, near_end)

    def z_far(k):
        return z_copy(4, far_end, k, near_end, src=xr_late, dst=xr_late)

    def link_half(link, first):
        return (0 if first else 1) if link == 0 else (1 if first else 0)

    links = (xn, yn)

    def own_copy(link, owner, i):
        k = link_half(link, i == 0)
        return remote(
            xc.at[r, part(k)], xc.at[owner, part(k)], ys.at[link, i], yr.at[link, i],
            links[link], c,
        )

    def pass_copy(link, owner):
        k = link_half(link, False)
        block = xc.at[owner, part(k)]
        return remote(block, block, ys.at[link, 2], yr.at[link, 2], links[link], c)

    def sib_copy(i, src, owner, k):
        dst = xc_late.at[part(k)] if i == 3 else xc.at[owner, part(k)]
        return remote(src, dst, ss.at[i, k], sr.at[i, k], sib, c)

    for k in range(2):
        for link in range(2):
            own_copy(link, r, k).start()
    for p in range(pairs):
        two = [xv[:, q * tile : (q + 1) * tile].astype(f32) for q in (p, p + pairs)]
        for h in range(2):
            rows = [b[h * some : (h + 1) * some] for b in two]
            xr[h, c, p] = jnp.concatenate(rows, axis=0).astype(bf16)

    for h in range(2):

        @pl.when(c < 3)
        def _():
            z_copy(0, c, h, c + 1).start()

        @pl.when(c > 0)
        def _():
            z_copy(1, c, h, c - 1).start()

    lax.fori_loop(0, groups, start_tiles, 0)
    for k in range(2):
        sib_copy(0, xc.at[r, part(k)], r, k).start()

    coords_v_copy.wait()
    count_copy.wait()
    rows_v, cols_v = coords_v[0, 0], coords_v[1, 0]
    lane = lax.broadcasted_iota(i32, (slots, slots), 1)
    down = lax.broadcasted_iota(i32, (slots, slots), 0)
    live = lax.broadcasted_iota(i32, (1, slots), 1) < count_v[0:1, 0:1]
    places = (rows_v % span, cols_v // span * per_slab + cols_v % per_slab)
    width = table_v.shape[1]
    order = lax.broadcasted_iota(i32, (slots, width), 0) + 1
    target = lax.broadcasted_iota(i32, (slots, width), 1)
    lates = (cols_v // span == late_col, rows_v % span // per_slab == late_row)

    def on_rows(values):
        wide = jnp.where(down == lane, jnp.broadcast_to(values, (slots, slots)), 0)
        return jnp.sum(wide.astype(f32), axis=1, keepdims=True).astype(i32)

    def count_of(mask):
        return jnp.sum(jnp.where(mask, 1.0, 0.0), axis=1, keepdims=True).astype(i32)

    for k in range(2):
        place = jnp.where(live, places[k], -1)
        late = jnp.where(live & lates[k], 1, 0)
        ahead = count_of((late == 0) & (lane < down))
        behind = count_of((late == 1) & (lane >= down))
        spot = jnp.where(on_rows(late) == 1, slots - behind, ahead)
        here = spot == lane
        table_v[4 + k : 5 + k, 0:slots] = jnp.max(
            jnp.where(here, down, 0), axis=0, keepdims=True
        )
        place = jnp.max(jnp.where(here, on_rows(place) + 1, 0), axis=0, keepdims=True) - 1
        tall = on_rows(place)
        before = jnp.where((tall == place) & (down < lane), down + 1, 0)
        table_v[2 * k : 2 * k + 1, 0:slots] = jnp.max(before, axis=0, keepdims=True)
        found = jnp.where(tall == target, order, 0)
        table_v[2 * k + 1 : 2 * k + 2, :] = jnp.max(found, axis=0, keepdims=True)
    table_copy.start()
    cum_f[0] = jnp.zeros(cum_f.shape[1:], f32)
    for h in range(2):
        cum_m[h, 0] = jnp.zeros(cum_m.shape[2:], f32)

    down = lax.broadcasted_iota(i32, (tile, tile), 0)
    over = lax.broadcasted_iota(i32, (tile, tile), 1)
    def clear_late(p, _):
        xc[late_col, p] = jnp.zeros(xc.shape[2:], bf16)
        xr[p // pairs, late_row, p % pairs] = jnp.zeros(xr.shape[3:], bf16)
        return 0

    lax.fori_loop(0, per_slab, clear_late, 0)
    tri[0] = (down >= over).astype(f32).astype(bf16)
    tri[1] = (down < over).astype(f32).astype(bf16)
    coords_copy.wait()

    def split_group(g, _):
        tile_copy(g).wait()
        for i in range(GROUP):
            s = g * GROUP + i
            gap = jnp.full((1, tile), coords[0, 0, 0, s] - coords[1, 0, 0, s], i32)
            off = jnp.minimum(gap * gap, 1).astype(f32).astype(bf16)
            stored = lower[s]
            upper[s] = stored.T * jnp.maximum(tri[0], off)
            lower[s] = stored * jnp.maximum(tri[1], off)
        return 0

    def split(a, b):
        lax.fori_loop(a * groups // 10, b * groups // 10, split_group, 0)

    def z_pass_one(k):
        @pl.when(mid)
        def _():
            z_copy(2, near_end, k, far_mid).wait_recv()
            z_inner(k).start()
            z_outer(k).wait_recv()
            z_outer(k).start()

    def z_pass_two(k):
        @pl.when(mid)
        def _():
            z_far(k).wait_recv()
            z_far(k).start()

    split(0, 2)
    for link in range(2):
        own_copy(link, links[link], 0).wait_recv()
        pass_copy(1 - link, links[link]).start()
        k = link_half(link, True)
        sib_copy(1 + link, xc.at[links[link], part(k)], links[link], k).start()
    z_pass_one(0)
    split(2, 5)
    for link in range(2):
        own_copy(link, links[link], 1).wait_recv()
        k = link_half(link, False)
        sib_copy(1 + link, xc.at[links[link], part(k)], links[link], k).start()
    z_pass_one(1)
    split(5, 8)
    z_pass_two(0)
    split(8, 10)
    for link in range(2):
        pass_copy(link, dn).wait_recv()
        k = link_half(link, False)
        sib_copy(3, xc.at[dn, part(k)], dn, k).start()
    z_pass_two(1)
    table_copy.wait()

    def sib_wait(i, owner):
        for k in range(2):
            sib_copy(i, xc.at[owner, part(k)], owner, k).wait_recv()

    for i, owner in enumerate((sib, 2 * beside + 1 - core, 2 * across + 1 - core)):
        sib_wait(i, owner)

    def running_sums(make, link, a, b):
        for n in range(a, b):
            make(n)
            if n - LAG >= a:
                link(n - LAG)
        for n in range(max(a, b - LAG), b):
            link(n)

    def forward(a, b):
        def make(n):
            s = table[4, n]
            col = coords[1, 0, 0, s]
            made[n] = jnp.dot(
                xc[lax.div(col, span), lax.rem(col, per_slab)], upper[s],
                preferred_element_type=f32,
            )

        def link(n):
            cum_f[n + 1] = made[n] + cum_f[table[0, n]]

        running_sums(make, link, a, b)

    def mirror(h, a, b):
        def row_of(n):
            return lax.rem(coords[0, 0, 0, table[5, n]], span)

        def make(n):
            row = row_of(n)
            out = jnp.dot(
                xr[h, lax.div(row, per_slab), lax.rem(row, pairs)], lower[table[5, n]],
                preferred_element_type=f32,
            )
            made_m[n, 0] = out[:some]
            made_m[n, 1] = out[some:]

        def link(n):
            side = lax.div(lax.rem(row_of(n), per_slab), pairs)
            cum_m[h, n + 1] = made_m[n, side] + cum_m[h, table[2, n]]

        running_sums(make, link, a, b)

    def pair(h, owner, p):
        first = owner * per_slab + p
        return jnp.concatenate(
            [cum_m[h, table[3, first]], cum_m[h, table[3, first + pairs]]], axis=0
        )

    def fill_pairs(dst, h, owner, lo, n, *more, to=0):
        def body(i, _):
            out = pair(h, owner, lo + i)
            for source, offset in more:
                out = out + source[offset + i].astype(f32)
            dst[to + i] = out.astype(dst.dtype)
            return 0

        lax.fori_loop(0, n, body, 0, unroll=8)

    def fill(dst, cum, at, owner, k, *more, to=None):
        base = k * half

        def body(i, _):
            out = cum[table[at, owner * per_slab + base + i]]
            for source, offset in more:
                out = out + source[offset + i].astype(f32)
            dst[(base if to is None else to) + i] = out.astype(dst.dtype)
            return 0

        lax.fori_loop(0, half, body, 0, unroll=8)

    def near(i, k):
        return remote(
            z_out.at[i, part(k)], z_in.at[i, part(k)], ps.at[i, k], pr.at[i, k], r, next_mid
        )

    def far(i, k):
        return remote(
            z_out.at[i, part(k)], z_in.at[3 + i, part(k)], ps.at[i, k], pr.at[3 + i, k],
            r, far_mid,
        )

    def to_end(k):
        return remote(
            z_out.at[2, part(k)], z_in.at[0, part(k)], ps.at[2, k], pr.at[0, k], r, near_end
        )

    def chain_far(i, k):
        @pl.when(mid)
        def _():
            near(i, k).wait_recv()
            owner = far_end if i == 0 else far_mid
            fill(z_out.at[i], cum_f, 1, owner, k, (z_in.at[i], k * half))
            far(i, k).start()

    def chain_end(k):
        @pl.when(mid)
        def _():
            far(0, k).wait_recv()
            fill(z_out.at[2], cum_f, 1, near_end, k, (z_in.at[3], k * half))
            to_end(k).start()

    def rows_of(k):
        return pl.ds(k * quarter, quarter)

    def to_sib(j, h):
        return remote(
            sib_out.at[h, j], sib_in.at[h, j], bs.at[j, h], br.at[j, h], sib, c
        )

    def diag(link, h):
        return remote(
            diag_out.at[h, link], diag_in.at[h, link], ds.at[link, h], dr.at[link, h],
            links[link], c,
        )

    def beside_copy(link, i, h):
        k = link_half(link, i == 0)
        return remote(
            near_out.at[h, link, rows_of(k)], near_in.at[h, link, rows_of(k)],
            ns.at[link, i, h], nr.at[link, i, h], links[link], c,
        )

    def give_sib(h):
        for j, to in enumerate((opposite, beside, across, chip)):
            fill_pairs(sib_out.at[h, j], h, 2 * to + 1 - core, 0, pairs)
            to_sib(j, h).start()

    def give_diag(h):
        to_sib(0, h).wait_recv()
        for link in range(2):
            lo = link * quarter
            fill_pairs(diag_out.at[h, link], h, dn, lo, quarter, (sib_in.at[h, 0], lo))
            diag(link, h).start()

    def give_first(h):
        for link in range(2):
            to_sib(1 + link, h).wait_recv()
            lo = link_half(link, True) * quarter
            fill_pairs(
                near_out.at[h, link], h, links[link], lo, quarter,
                (sib_in.at[h, 1 + link], lo), to=lo,
            )
            beside_copy(link, 0, h).start()

    def give_second(h):
        for link in range(2):
            diag(1 - link, h).wait_recv()
            lo = link_half(link, False) * quarter
            fill_pairs(
                near_out.at[h, link], h, links[link], lo, quarter,
                (sib_in.at[h, 1 + link], lo), (diag_in.at[h, 1 - link], 0), to=lo,
            )
            beside_copy(link, 1, h).start()

    def lanes(p):
        return pl.ds(pl.multiple_of(p * tile, tile), tile)

    def put(h, p, out, keep):
        rows = pl.ds(h * some, some)
        for q, value in ((p, out[:some]), (p + pairs, out[some:])):
            o_ref[rows, lanes(q)] = o_ref[rows, lanes(q)] + value if keep else value

    def base():
        for h in range(2):
            to_sib(3, h).wait_recv()

        def body(p, _):
            at = c * per_slab + p
            whole = (cum_f[table[1, at]], cum_f[table[1, at + pairs]])
            for h in range(2):
                rows = [b[h * some : (h + 1) * some] for b in whole]
                out = jnp.concatenate(rows, axis=0) + pair(h, r, p)
                put(h, p, out + sib_in[h, 3, p].astype(f32), False)
            return 0

        lax.fori_loop(0, pairs, body, 0, unroll=4)

    def add(k, *sources):
        def body(p, _):
            at = lanes(k * half + p)
            out = o_ref[:, at]
            for source in sources:
                out = out + source[k * half + p].astype(f32)
            o_ref[:, at] = out
            return 0

        lax.fori_loop(0, half, body, 0, unroll=8)

    def take(i, h):
        for link in range(2):
            beside_copy(link, i, h).wait_recv()
            lo = link_half(link, i == 0) * quarter

            def body(p, _):
                put(h, lo + p, near_in[h, link, lo + p].astype(f32), True)
                return 0

            lax.fori_loop(0, quarter, body, 0, unroll=8)

    def late_here(h):
        def body(p, _):
            xr[h, late_row, p] = xr_late[h, p]
            return 0

        lax.fori_loop(0, pairs, body, 0, unroll=8)

    early_f, early_m = slots - LATE_COLS, slots - LATE_ROWS
    forward(0, early_f)
    sib_wait(3, late_col)

    def fetch(p, _):
        xc[late_col, p] = xc_late[p]
        return 0

    lax.fori_loop(0, per_slab, fetch, 0, unroll=8)
    forward(early_f, slots)

    @pl.when(end)
    def _():
        for i, owner in enumerate((3 - c, 3 - next_mid, next_mid)):
            for k in range(2):
                fill(z_out.at[i], cum_f, 1, owner, k)
                near(i, k).start()
        for owner in (next_mid, 3 - next_mid):
            for h in range(2):
                z_copy(0, owner, h, next_mid).wait_recv()

    for h in range(2):
        mirror(h, 0, early_m)

    def finish_mirror(h):
        @pl.when(end)
        def _():
            z_copy(0, late_row, h, next_mid, dst=xr_late).wait_recv()

        late_here(h)
        mirror(h, early_m, slots)
        give_sib(h)

    finish_mirror(0)
    finish_mirror(1)
    chain_far(0, 0)
    give_diag(0)
    give_diag(1)
    chain_far(0, 1)
    give_first(0)
    give_first(1)
    chain_end(0)
    give_second(0)
    give_second(1)
    chain_far(1, 0)
    chain_end(1)
    base()
    for k in range(2):

        @pl.when(c < 3)
        def _():
            z_copy(0, c, k, c + 1).wait_send()

        @pl.when(c > 0)
        def _():
            z_copy(1, c, k, c - 1).wait_send()

        @pl.when(mid)
        def _():
            z_inner(k).wait_send()
            z_outer(k).wait_send()
            z_far(k).wait_send()

        for link in range(2):
            own_copy(link, r, k).wait_send()
        for i, owner in enumerate((r, xn, yn, dn)):
            sib_copy(i, xc.at[owner, part(k)], owner, k).wait_send()
    for link in range(2):
        pass_copy(link, links[1 - link]).wait_send()

    @pl.when(end)
    def _():
        for k in range(2):
            to_end(k).wait_recv()
            add(k, z_in.at[0])

    chain_far(1, 1)
    for h in range(2):
        for i in range(2):
            take(i, h)

    @pl.when(mid)
    def _():
        for k in range(2):
            far(1, k).wait_recv()
            near(2, k).wait_recv()
            add(k, z_in.at[4], z_in.at[2])

    for i in range(3):
        for k in range(2):
            near(i, k).wait_send()
    for h in range(2):
        for link in range(2):
            diag(link, h).wait_send()
            for i in range(2):
                beside_copy(link, i, h).wait_send()
        for j in range(4):
            to_sib(j, h).wait_send()


def fused(tiles, tile_coords, tile_counts, x):
    slots, tile = tiles.shape[2], tiles.shape[-1]
    vecs, width = x.shape
    slab = width // tile
    pairs, some = slab // 2, vecs // 2
    dma, bf16, f32, i32 = pltpu.SemaphoreType.DMA, jnp.bfloat16, jnp.float32, jnp.int32

    def blocks(*lead, dtype=bf16):
        return pltpu.VMEM((*lead, vecs, tile), dtype)

    return pl.pallas_call(
        fused_kernel,
        out_shape=jax.ShapeDtypeStruct(x.shape, f32),
        in_specs=[pl.BlockSpec(memory_space=pltpu.HBM)] * 4,
        out_specs=pl.BlockSpec(memory_space=pltpu.VMEM),
        scratch_shapes=[
            pltpu.VMEM(x.shape, bf16),
            blocks(2, 4, pairs),
            blocks(8, slab),
            blocks(2, pairs),
            blocks(slab),
            pltpu.VMEM((slots, tile, tile), bf16),
            pltpu.VMEM((slots, tile, tile), bf16),
            pltpu.VMEM((2, tile, tile), bf16),
            blocks(slots, dtype=f32),
            pltpu.VMEM((slots, 2, some, tile), f32),
            blocks(slots + 1, dtype=f32),
            pltpu.VMEM((2, slots + 1, some, tile), f32),
            pltpu.VMEM((8, 8 * slab), i32),
            blocks(3, slab),
            blocks(5, slab),
            blocks(2, 4, pairs),
            blocks(2, 4, pairs),
            blocks(2, 2, pairs // 2),
            blocks(2, 2, pairs // 2),
            blocks(2, 2, pairs),
            blocks(2, 2, pairs),
            pltpu.SMEM(tile_coords.shape, i32),
            pltpu.VMEM(tile_coords.shape, i32),
            pltpu.VMEM((1, 1), i32),
            pltpu.SMEM((8, 8 * slab), i32),
            dma((5,)),
            dma((slots // GROUP,)),
            dma((5, 2)), dma((4, 2)),
            dma((2, 3)), dma((2, 3)),
            dma((4, 2)), dma((4, 2)),
            dma((3, 2)), dma((5, 2)),
            dma((4, 2)), dma((4, 2)),
            dma((2, 2)), dma((2, 2)),
            dma((2, 2, 2)), dma((2, 2, 2)),
        ],
        compiler_params=pltpu.CompilerParams(
            collective_id=0, has_side_effects=True, vmem_limit_bytes=VMEM_LIMIT
        ),
        name="fused_product",
    )(
        pltpu.with_memory_space_constraint(tile_coords, pltpu.HBM), tile_counts,
        pltpu.with_memory_space_constraint(x, pltpu.HBM), tiles,
    )


def apply_kernel(
    slots, tile, per_slab, n_cols, coords, count,
    t_ref, xr_ref, xc_ref, f_ref, m_ref, facc, macc,
):
    step = pl.program_id(0)
    group = t_ref.shape[2]

    @pl.when(step == 0)
    def _():
        facc[...] = jnp.zeros_like(facc)
        macc[...] = jnp.zeros_like(macc)

    def place(s):
        tile_row, tile_col = coords[s], coords[slots + s]
        local = tile_row % (per_slab * n_cols)
        row_at = (local // per_slab, pl.multiple_of(local % per_slab * tile, tile))
        col_at = (
            tile_col // (per_slab * n_cols), pl.multiple_of(tile_col % per_slab * tile, tile),
        )
        return row_at, col_at

    def run(masked):
        made = []
        for g in range(group):
            s = step * group + g
            (ro, rp), (co, cp) = place(s)
            x_row = xr_ref[ro, :, pl.ds(rp, tile)]
            x_col = xc_ref[co, :, pl.ds(cp, tile)]
            upper = lower = t_ref[0, 0, g]
            if masked:
                off = coords[s] != coords[slots + s]
                down = lax.broadcasted_iota(jnp.int32, (tile, tile), 0)
                down = jnp.where(off, -1, down)
                across = lax.broadcasted_iota(jnp.int32, (tile, tile), 1)
                stored = upper.astype(jnp.float32)
                upper = jnp.where(down <= across, stored, 0.0).astype(jnp.bfloat16)
                lower = jnp.where(down < across, stored, 0.0).astype(jnp.bfloat16)
            forward = lax.dot_general(
                x_col, upper, (((1,), (1,)), ((), ())), preferred_element_type=jnp.float32
            )
            mirror = lax.dot_general(
                x_row, lower, (((1,), (0,)), ((), ())), preferred_element_type=jnp.float32
            )
            if masked:
                live = s < count[0]
                forward = jnp.where(live, forward, 0.0)
                mirror = jnp.where(live, mirror, 0.0)
            made.append((forward, mirror))
        for g in range(group):
            (ro, rp), (co, cp) = place(step * group + g)
            forward, mirror = made[g]
            facc[ro, :, pl.ds(rp, tile)] += forward
            macc[co, :, pl.ds(cp, tile)] += mirror

    special = coords[step * group] == coords[slots + step * group]
    for g in range(1, group):
        s = step * group + g
        special = special | (coords[s] == coords[slots + s])
    special = special | (step * group + group > count[0])

    @pl.when(special)
    def _():
        run(True)

    @pl.when(jnp.logical_not(special))
    def _():
        run(False)

    @pl.when(step == pl.num_programs(0) - 1)
    def _():
        f_ref[...] = facc[...].astype(f_ref.dtype)
        m_ref[...] = macc[...].astype(m_ref.dtype)


def apply_tiles(tiles, coords, count, xr, xc, tile):
    slots = tiles.shape[2]
    group = GROUP if slots % GROUP == 0 else 1
    n_cols = xr.shape[0]
    per_slab = xr.shape[2] // tile
    whole = lambda a: pl.BlockSpec(a.shape, lambda i, *_: (0, 0, 0))
    return pl.pallas_call(
        functools.partial(apply_kernel, slots, tile, per_slab, n_cols),
        out_shape=(
            jax.ShapeDtypeStruct(xr.shape, jnp.bfloat16),
            jax.ShapeDtypeStruct(xc.shape, jnp.bfloat16),
        ),
        grid_spec=pltpu.PrefetchScalarGridSpec(
            num_scalar_prefetch=2,
            grid=(slots // group,),
            in_specs=[
                pl.BlockSpec((1, 1, group, tile, tile), lambda i, *_: (0, 0, i, 0, 0)),
                whole(xr),
                whole(xc),
            ],
            out_specs=(whole(xr), whole(xc)),
            scratch_shapes=[
                pltpu.VMEM(xr.shape, jnp.float32),
                pltpu.VMEM(xc.shape, jnp.float32),
            ],
        ),
        compiler_params=pltpu.CompilerParams(vmem_limit_bytes=VMEM_LIMIT),
        name="apply_tiles",
    )(coords, count, tiles, xr, xc)


def shards(n_rows, n_cols, tiles, tile_coords, tile_counts, vectors):
    tile = tiles.shape[-1]
    x = vectors.T
    if (n_rows, n_cols) == (8, 4):
        return fused(tiles, tile_coords, tile_counts, x).T
    coords, count = tile_coords.reshape(-1), tile_counts.reshape(-1)
    xr = lax.all_gather(x, "col", axis=0)
    xc = lax.all_gather(x, "row", axis=0)
    f, m = apply_tiles(tiles, coords, count, xr, xc, tile)
    f = lax.all_to_all(f, "col", 0, 0, tiled=True)
    m = lax.all_to_all(m, "row", 0, 0, tiled=True)
    return (jnp.sum(f.astype(jnp.float32), 0) + jnp.sum(m.astype(jnp.float32), 0)).T


def solution(mesh):
    in_specs = (
        P("row", "col", None, None, None),
        P(None, "row", "col", None),
        P("row", "col"),
        P(("row", "col"), None),
    )
    out_specs = P(("row", "col"), None)
    body = functools.partial(shards, mesh.shape["row"], mesh.shape["col"])
    return jax.shard_map(body, mesh=mesh, in_specs=in_specs, out_specs=out_specs, check_vma=False)
```
